256 devices in a mesh: prow: 32 (over x, y, core), pcol: 8 (over z).
Axes of the slice: x: 4, y: 4, z: 8, core: 2. Of those that a mesh axis runs over, the one named last changes fastest.
Arguments:
- right_sides: bfloat16 [4, 32, 256, 256], P(None, 'prow'), may hold values from -6 to 6
- lower_diag_inverse: bfloat16 [4, 32, 256, 256], P(None, 'prow'), may hold values from -1 to 2, as said below
- upper_diag_inverse: bfloat16 [4, 32, 256, 256], P(None, 'prow'), may hold values from -1 to 2, as said below
- lower_blocks: bfloat16 [6, 32, 32, 256, 256], P(None, 'prow', 'pcol'), may hold values from -0.375 to 0.375
- upper_blocks: bfloat16 [6, 32, 32, 256, 256], P(None, 'prow', 'pcol'), may hold values from -0.375 to 0.375
- block_mask: int32 [6, 32, 32], replicated, may hold values from 0 to 1, as said below
Outputs:
- solution: bfloat16 [4, 32, 256, 256], P(None, 'prow')
The draws below stay inside these ranges and needn't reach their ends.
Inputs may be any that keep to these rules, and one draw needn't show every extreme that they name: Each supernode of a level has one parent on the next level; block_mask[p, i, j] is 1 exactly when supernode i of level h is the ancestor of supernode j of level g, else 0. Every supernode has exactly one ancestor on each higher level; supernodes differ in how many descendants they have. `lower_diag_inverse`: identity plus a dense part. `upper_diag_inverse`: identity plus a dense part.
All inputs are finite; a program needn't handle non-finite values.
Results may differ from the reference program's by a relative error of at most 0.03.
Values may be sent and summed in bfloat16 or wider, within the bound.
A program may use at most 64 MiB of HBM per device.

```python
import jax
import jax.numpy as jnp

B = 256
RHS = 256
LEV = 4
S = 32
NPAIR = 6


def inverse_draw(key):
    dense = jax.random.normal(key, (LEV, S, B, B), jnp.float32) * (0.35 / B ** 0.5)
    dense = jnp.clip(dense, -1.0, 1.0)
    return (dense + jnp.eye(B, dtype=jnp.float32)).astype(jnp.bfloat16)


def draw_lower_diag_inverse(key, part):
    key = jax.random.fold_in(key, 11)
    return inverse_draw(key)


def draw_upper_diag_inverse(key, part):
    key = jax.random.fold_in(key, 23)
    return inverse_draw(key)


def draw_block_mask(key, part):
    key = jax.random.fold_in(key, 37)
    parents = jax.random.randint(key, (LEV - 1, S), 0, S).astype(jnp.int32)
    members = jnp.arange(S, dtype=jnp.int32)
    layers = []
    for tree_height in range(LEV):
        for lower_neighbor in range(tree_height):
            ancestor = members
            for level in range(lower_neighbor, tree_height):
                ancestor = jnp.take(parents[level], ancestor)
            layers.append((ancestor[None, :] == members[:, None]).astype(jnp.int32))
    return jnp.stack(layers)


def levels(key, shape, cuts, least, largest):
    gain = 1.0
    for axis_at, parts in cuts:
        steps = jax.random.uniform(jax.random.fold_in(jax.random.fold_in(key, 6), axis_at), (parts,), jnp.float32, least / len(cuts), largest / len(cuts))
        gain = gain * jnp.repeat(jnp.exp(steps), shape[axis_at] // parts).reshape((-1,) + (1,) * (len(shape) - 1 - axis_at))
    return gain


def gaussian(key, extent, spread, reach, pieces=(), held_as=jnp.bfloat16):
    factor_of = levels(key, extent, pieces, -0.22, 0.18) if pieces else 1.0
    drawn = jax.random.normal(key, extent, jnp.float32) * spread * factor_of
    return jnp.minimum(jnp.maximum(drawn, -reach), reach).astype(held_as)


def setup_inputs(seed: int = 0) -> dict:
    seeds = jax.random.split(jax.random.key(seed), 7)
    return {
        "right_sides": gaussian(seeds[0], (LEV, S, B, RHS), 1.0, 6.0, ((1, 32),)),
        "lower_diag_inverse": draw_lower_diag_inverse(jax.random.fold_in(seeds[6], 71), 0),
        "upper_diag_inverse": draw_upper_diag_inverse(jax.random.fold_in(seeds[6], 71), 0),
        "lower_blocks": gaussian(seeds[3], (NPAIR, S, S, B, B), B ** -0.5, 0.375, ((1, 32), (2, 8))),
        "upper_blocks": gaussian(seeds[4], (NPAIR, S, S, B, B), B ** -0.5, 0.375, ((1, 32), (2, 8))),
        "block_mask": draw_block_mask(jax.random.fold_in(seeds[6], 71), 0),
    }


def reference(right_sides, lower_diag_inverse, upper_diag_inverse, lower_blocks, upper_blocks, block_mask):
    mask_f = block_mask.astype(jnp.float32)
    forward_entries = []
    for tree_height in range(LEV):
        pending_updates = jnp.zeros((S, B, RHS), jnp.float32)
        for lower_neighbor in range(tree_height):
            pair_slot = tree_height * (tree_height - 1) // 2 + lower_neighbor
            masked_entries = lower_blocks[pair_slot].astype(jnp.float32) * mask_f[pair_slot][:, :, None, None]
            pending_updates = pending_updates + jnp.einsum('cwhe,wev->chv', masked_entries, forward_entries[lower_neighbor].astype(jnp.float32))
        residual_rows = (right_sides[tree_height].astype(jnp.float32) - pending_updates).astype(jnp.bfloat16)
        solved_rows = jnp.einsum('jqt,jtw->jqw', lower_diag_inverse[tree_height].astype(jnp.float32), residual_rows.astype(jnp.float32))
        forward_entries.append(solved_rows.astype(jnp.bfloat16))
    backward_entries = [None] * LEV
    for tree_height in range(LEV - 1, -1, -1):
        pending_updates = jnp.zeros((S, B, RHS), jnp.float32)
        for upper_neighbor in range(tree_height + 1, LEV):
            pair_slot = upper_neighbor * (upper_neighbor - 1) // 2 + tree_height
            masked_entries = upper_blocks[pair_slot].astype(jnp.float32) * jnp.transpose(mask_f[pair_slot])[:, :, None, None]
            pending_updates = pending_updates + jnp.einsum('cwhe,wev->chv', masked_entries, backward_entries[upper_neighbor].astype(jnp.float32))
        residual_rows = (forward_entries[tree_height].astype(jnp.float32) - pending_updates).astype(jnp.bfloat16)
        solved_rows = jnp.einsum('jqt,jtw->jqw', upper_diag_inverse[tree_height].astype(jnp.float32), residual_rows.astype(jnp.float32))
        backward_entries[tree_height] = solved_rows.astype(jnp.bfloat16)
    return jnp.stack(backward_entries)
```

```python
import functools

import jax
import jax.numpy as jnp
from jax import lax
from jax.experimental import pallas as pl
from jax.experimental.pallas import tpu as pltpu
from jax.sharding import PartitionSpec as P

MESH = pl.DeviceIdType.MESH
F32 = jnp.float32
BF16 = jnp.bfloat16
B = 256
LEV = 4
NPAIR = 6
CHIPS = 16
NZ = 8
W = 16
FIRST = (0, 1, 3)
MOVED = (2, 5, 4)
UORD = (5, 2, 4, 0, 1, 3)
UROW = (2, 1, 1, 0, 0, 0)
ROW_OF = (1, 2, 2, 3, 3, 3)
UGROUPS = ((0, 1), (1, 3), (3, 6))


def dot_nt(a, b):
    return lax.dot_general(a, b, (((1,), (1,)), ((), ())), preferred_element_type=F32)


def kernel(
    rhs_hbm, linv_hbm, uinv_hbm, lower_hbm, upper_hbm, mask,
    out_hbm,
    rhs, linv, uinv, lower, upper,
    g_all, g_home, home, x0, first_m, part, zsum,
    mov, mov_sib, comb, rs_buf, piece, lact,
    ucand, ur_buf, upiece, uact0, uact1, uact2,
    fv, u_src, u21, u32, u31,
    sol, s3, s2, s1, out_buf, out_t,
    load_sem, send_sem, recv_sem,
):
    row = lax.axis_index("prow")
    z = lax.axis_index("pcol")
    q = row // 2
    core = row % 2
    other = 1 - core

    def dev(chip, c, zz):
        return (chip * 2 + c, zz)

    sibling = dev(q, other, z)

    loads = {}
    n_load = [0]

    def load(name, src, dst):
        copy = pltpu.make_async_copy(src, dst, load_sem.at[n_load[0]])
        n_load[0] += 1
        copy.start()
        loads[name] = copy

    load("linv", linv_hbm.at[:, 0], linv)
    load("rhs", rhs_hbm.at[:, 0], rhs)
    for p in (2, 0, 5, 4, 1, 3):
        load(("l", p), lower_hbm.at[p, 0], lower.at[p])
    load("uinv", uinv_hbm.at[:, 0], uinv.at[core])
    load("upper", upper_hbm.at[:, 0], upper)

    plane = q // 2
    x, y, qb = q // 4, q % 4, q % 2
    turn = (z - plane + 9) % 8
    flag = 1 - turn // 4
    hx = (x + 3 + 2 * (1 - flag) - turn + 8) % 4
    hy = (y + flag * (2 * qb - 1) + 4) % 4
    home_chip = hx * 4 + hy
    dx = (x - z // 2 + 4) % 4
    dy = (y - 2 * (z % 2) + 4) % 4
    src_qb = ((dy + 1) % 4) // 2
    src_v = 1 - dy // 2
    src_turn = 4 * src_v + (3 + 2 * src_v - dx + 4) % 4
    src_z = (src_turn + 7 + z) % 8
    src_chip = 2 * z + src_qb
    slot = src_qb * 8 + src_z

    barrier = pltpu.get_barrier_semaphore()

    def greet(device):
        pl.semaphore_signal(barrier, inc=1, device_id=device, device_id_type=MESH)

    def greet_plane(d, _):
        greet(dev((q + d) % CHIPS, core, z))
        return 0

    def greet_z(d, _):
        greet(dev(q, core, (z + d) % NZ))
        return 0

    def greet_cross(d, _):
        greet(dev(q, other, (z + d) % NZ))
        return 0

    move_src = (q // 2, q % 2)

    def greet_move(d, _):
        greet(dev((q + d) % CHIPS, move_src[1], move_src[0]))
        return 0

    own_move = jnp.logical_and(z == q // 2, core == q % 2)
    greet(dev(src_chip, core, src_z))
    greet(dev(src_chip, other, src_z))
    lax.fori_loop(0, NZ, greet_cross, 0)
    lax.fori_loop(1, CHIPS, greet_plane, 0)
    lax.fori_loop(1, NZ, greet_z, 0)
    lax.fori_loop(1, CHIPS, greet_move, 0)

    @pl.when(jnp.logical_not(own_move))
    def _():
        greet(dev(q, move_src[1], move_src[0]))

    sent = []

    def remote(src, dst, sem, device):
        pltpu.make_async_remote_copy(
            src_ref=src, dst_ref=dst, send_sem=send_sem.at[sem], recv_sem=recv_sem.at[sem],
            device_id=device, device_id_type=MESH,
        ).start()

    def wait_recv(sem, ref):
        pltpu.make_async_copy(ref, ref, recv_sem.at[sem]).wait()

    sems = {}

    def new_sem(name):
        sems[name] = len(sems)
        return sems[name]

    def to_sibling(name, src, dst):
        sem = new_sem(name)
        remote(src, dst, sem, sibling)
        sent.append((sem, src))

    def plane_gather(name, src, buf, at):
        sem = new_sem(name)

        def body(d, _):
            remote(src, buf.at[at], sem, dev((q + d) % CHIPS, core, z))
            return 0

        lax.fori_loop(1, CHIPS, body, 0)
        buf[at] = src[...]
        sent.append((sem, buf.at[pl.ds(0, 15)] if len(buf.shape) == 4 else buf.at[pl.ds(0, 30)]))

    def plane_wait(name, buf):
        wait_recv(sems[name], buf.at[pl.ds(0, 15)] if len(buf.shape) == 4 else buf.at[pl.ds(0, 30)])

    def z_exchange(name, src_of, buf, at):
        sem = new_sem(name)

        def body(d, _):
            zz = (z + d) % NZ
            remote(src_of(zz), buf.at[at], sem, dev(q, core, zz))
            return 0

        lax.fori_loop(1, NZ, body, 0)
        sent.append((sem, buf.at[pl.ds(0, 7)]))

    loads["linv"].wait()
    loads["rhs"].wait()

    def make_g(h):
        g_all[h] = jnp.dot(linv[h], rhs[h], preferred_element_type=F32).T.astype(BF16)

    def make_m(p, dst, first):
        if first:
            loads[("l", p)].wait()
        for k in range(4):
            weight = mask[p, row, 4 * z + k].astype(F32)
            dst[k] = (jnp.dot(linv[ROW_OF[p]], lower[p, k], preferred_element_type=F32) * weight).astype(BF16)

    make_g(0)
    make_m(2, mov.at[0], True)
    make_m(0, first_m.at[core, 0], True)
    pl.semaphore_wait(barrier, 48 - own_move.astype(jnp.int32))

    sem = new_sem("home")
    mine = pl.ds(pl.multiple_of(core * 128 + z * W, W), W)
    yours = pl.ds(pl.multiple_of(other * 128 + z * W, W), W)
    remote(g_all.at[0, mine], home.at[core], sem, dev(home_chip, core, plane))
    remote(g_all.at[0, yours], home.at[core], sem, dev(home_chip, other, plane))
    sent.append((sem, home))

    def move_to_sibling(i):
        to_sibling(("mov", i), mov.at[i, pl.ds(2 * other, 2)], mov_sib.at[i])

    move_to_sibling(0)
    to_sibling(("m", 0), first_m.at[core, 0], first_m.at[core, 0])

    for h in range(1, LEV):
        make_g(h)
    to_sibling("g", g_all.at[:, yours], g_home.at[core])
    g_home[core] = g_all[:, mine]

    for i in (1, 2):
        make_m(MOVED[i], mov.at[i], True)
        move_to_sibling(i)

    def combine(i):
        wait_recv(sems[("mov", i)], mov_sib.at[i])
        for e in range(2):
            comb[i, e] = mov[i, 2 * core + e] + mov_sib[i, e]
        sem = new_sem(("rs", i))

        def body(d, _):
            chip = (q + d) % CHIPS
            rows = pl.ds(pl.multiple_of(chip * W, W), W)
            remote(comb.at[i, :, rows], rs_buf.at[i, q], sem, dev(chip, core, z))
            return 0

        lax.fori_loop(1, CHIPS, body, 0)
        rs_buf[i, q] = comb[i, :, pl.ds(pl.multiple_of(q * W, W), W)]
        sent.append((sem, rs_buf.at[i, pl.ds(0, 15)]))

    combine(0)

    wait_recv(sems["home"], home)
    plane_gather("x0", home, x0, slot)

    for i in (1, 2):
        make_m(FIRST[i], first_m.at[core, i], True)
        to_sibling(("m", i), first_m.at[core, i], first_m.at[core, i])
    combine(1)
    combine(2)

    def spread(i):
        wait_recv(sems[("rs", i)], rs_buf.at[i, pl.ds(0, 15)])
        total = rs_buf[i, 0].astype(F32)
        for s in range(1, CHIPS):
            total = total + rs_buf[i, s].astype(F32)
        piece[i] = total.astype(BF16)
        sem = new_sem(("lact", i))
        chip = 2 * z + core

        def body(t, _):
            remote(piece.at[i], lact.at[i, q], sem, dev(chip, (core + t) % 2, (z + t // 2) % NZ))
            return 0

        lax.fori_loop(1, 16, body, 0)

        @pl.when(own_move)
        def _():
            lact[i, q] = piece[i]

        @pl.when(jnp.logical_not(own_move))
        def _():
            remote(piece.at[i], lact.at[i, q], sem, dev(chip, core, z))

        return sem

    def wait_moved(sem_ref, i):
        @pl.when(own_move)
        def _():
            ref = lact.at[i, pl.ds(0, 15)]
            pltpu.make_async_copy(ref, ref, sem_ref).wait()

        @pl.when(jnp.logical_not(own_move))
        def _():
            ref = lact.at[i]
            pltpu.make_async_copy(ref, ref, sem_ref).wait()

    spread_sems = [spread(0)]

    loads["uinv"].wait()
    to_sibling("uinv", uinv.at[core], uinv.at[core])
    loads["upper"].wait()
    for n, p in enumerate(UORD):
        found = jnp.int32(0)
        at = jnp.int32(0)
        for k in range(4):
            bit = mask[p, 4 * z + k, row]
            found = found + bit
            at = at + k * bit
        block = jnp.dot(uinv[core, UROW[n]], upper[p, at], preferred_element_type=F32) * found.astype(F32)
        ucand[n] = block.astype(BF16)

    plane_wait("x0", x0)

    def products(i):
        wait_recv(sems[("m", i)], first_m.at[0, 0])
        for e in range(2):
            total = None
            for k in range(4):
                cols = x0[8 * (k // 2):8 * (k // 2) + 8, k % 2].reshape(128, B)
                term = dot_nt(cols, first_m[e, i, k])
                total = term if total is None else total + term
            part[i, :, e] = total.astype(BF16).reshape(NZ, W, B)
        z_exchange(("z", i), lambda zz: part.at[i, zz], zsum.at[i], z)
        zsum[i, z] = part[i, z]

    products(0)
    products(1)
    products(2)
    spread_sems.append(spread(1))
    spread_sems.append(spread(2))

    sem = new_sem("ur")

    def ur_body(d, _):
        zz = (z + d) % NZ
        rows = pl.ds(pl.multiple_of(zz * 32, 32), 32)
        remote(ucand.at[:, rows], ur_buf.at[z], sem, dev(q, core, zz))
        return 0

    lax.fori_loop(1, NZ, ur_body, 0)
    ur_buf[z] = ucand[:, pl.ds(pl.multiple_of(z * 32, 32), 32)]
    sent.append((sem, ur_buf.at[pl.ds(0, 7)]))

    def z_total(i):
        wait_recv(sems[("z", i)], zsum.at[i, pl.ds(0, 7)])
        total = zsum[i, 0].astype(F32)
        for s in range(1, NZ):
            total = total + zsum[i, s].astype(F32)
        return total

    def pushed(i, buf, p):
        def body(t, carry):
            for j in [t * 8 + u for u in range(8)]:
                val = buf[j].astype(F32)
                carry = tuple(carry[e] + val * mask[p, 2 * q + e, j].astype(F32) for e in range(2))
            return carry

        zero = jnp.zeros((W, B), F32)
        return lax.fori_loop(0, 4, body, (zero, zero))

    def push(name, level, i, slot_, buf):
        for e in range(2):
            block = lact[i, :, e].reshape(B, B)
            u_src[slot_, e] = dot_nt(fv[level, e], block).astype(BF16)
        plane_gather(name, u_src.at[slot_], buf, pl.ds(2 * q, 2))

    wait_recv(sems["g"], g_home.at[0])
    base = z_total(0)
    for e in range(2):
        fv[0, e] = g_home[e, 0]
        fv[1, e] = (g_home[e, 1].astype(F32) - base[e]).astype(BF16)
    wait_moved(recv_sem.at[spread_sems[0]], 0)
    push("u21", 1, 0, 0, u21)

    wait_moved(recv_sem.at[spread_sems[2]], 2)
    push("u31", 1, 2, 1, u31)

    wait_recv(sems["ur"], ur_buf.at[pl.ds(0, 7)])
    total = ur_buf[0].astype(F32)
    for s in range(1, NZ):
        total = total + ur_buf[s].astype(F32)
    upiece[...] = total.astype(BF16)
    uacts = (uact0, uact1, uact2)

    def spread_upper(n):
        lo, hi = UGROUPS[n]
        uact = uacts[n]
        sem = new_sem(("ua", n))

        def body(d, _):
            remote(upiece.at[pl.ds(lo, hi - lo)], uact.at[core, z], sem, dev(q, core, (z + d) % NZ))
            return 0

        lax.fori_loop(1, NZ, body, 0)
        uact[core, z] = upiece[lo:hi]
        sent.append((sem, uact.at[0, pl.ds(0, 7)]))

    def pass_upper(n):
        wait_recv(sems[("ua", n)], uacts[n].at[0, pl.ds(0, 7)])
        to_sibling(("us", n), uacts[n].at[core], uacts[n].at[core])

    def upper_ready(n):
        wait_recv(sems[("us", n)], uacts[n].at[0])

    for n in range(3):
        spread_upper(n)

    plane_wait("u21", u21)
    low, high = pushed(0, u21, 2)
    base = g_home[:, 2].astype(F32) - z_total(1)
    fv[2, 0] = (base[0] - low).astype(BF16)
    fv[2, 1] = (base[1] - high).astype(BF16)
    wait_moved(recv_sem.at[spread_sems[1]], 1)
    push("u32", 2, 1, 2, u32)

    base = g_home[:, 3].astype(F32) - z_total(2)
    plane_wait("u31", u31)
    low1, high1 = pushed(1, u31, 4)
    pass_upper(0)
    plane_wait("u32", u32)
    low, high = pushed(1, u32, 5)
    fv[3, 0] = (base[0] - low1 - low).astype(BF16)
    fv[3, 1] = (base[1] - high1 - high).astype(BF16)

    wait_recv(sems["uinv"], uinv.at[0])

    def own_term(level, e):
        return dot_nt(fv[level, e], uinv[e, level])

    def above(buf, n):
        group = sum(n >= lo for lo, _ in UGROUPS) - 1
        p = UORD[n]

        def body(t, chosen):
            for j in [t * 8 + u for u in range(8)]:
                val = buf[j].astype(F32)
                chosen = tuple(jnp.where(mask[p, j, 2 * q + e] == 1, val, chosen[e]) for e in range(2))
            return chosen

        zero = jnp.zeros((W, B), F32)
        chosen = lax.fori_loop(0, 4, body, (zero, zero))
        blocks = [uacts[group][e, :, n - UGROUPS[group][0]].reshape(B, B) for e in range(2)]
        return [dot_nt(chosen[e].astype(BF16), blocks[e]) for e in range(2)]

    def publish(level, buf):
        if buf is not None:
            plane_gather(("s", level), sol.at[level], buf, pl.ds(2 * q, 2))
        sem = new_sem(("out", level))
        at = core * 8 + z

        def body(d, _):
            remote(sol.at[level, core], out_buf.at[level, at], sem, dev(q, core, (z + d) % NZ))
            return 0

        def cross(d, _):
            remote(sol.at[level, other], out_buf.at[level, at], sem, dev(q, other, (z + d) % NZ))
            return 0

        lax.fori_loop(1, NZ, body, 0)
        lax.fori_loop(0, NZ, cross, 0)
        out_buf[level, at] = sol[level, core]
        sent.append((sem, out_buf.at[level, pl.ds(0, 15)]))

    stores = []

    def finish(level):
        wait_recv(sems[("out", level)], out_buf.at[level, pl.ds(0, 15)])
        out_t[level] = out_buf[level].reshape(B, B).astype(F32).T.astype(BF16)
        copy = pltpu.make_async_copy(out_t.at[level], out_hbm.at[level, 0], load_sem.at[n_load[0]])
        n_load[0] += 1
        copy.start()
        stores.append(copy)

    for e in range(2):
        sol[3, e] = own_term(3, e).astype(BF16)
    publish(3, s3)
    pass_upper(1)
    rest = [own_term(2, e) for e in range(2)]
    upper_ready(0)
    plane_wait(("s", 3), s3)
    terms = above(s3, 0)
    for e in range(2):
        sol[2, e] = (rest[e] - terms[e]).astype(BF16)
    publish(2, s2)
    pass_upper(2)
    upper_ready(1)
    terms = above(s3, 2)
    rest = [own_term(1, e) - terms[e] for e in range(2)]
    finish(3)
    plane_wait(("s", 2), s2)
    terms = above(s2, 1)
    for e in range(2):
        sol[1, e] = (rest[e] - terms[e]).astype(BF16)
    publish(1, s1)
    upper_ready(2)
    terms = above(s3, 5)
    more = above(s2, 4)
    rest = [own_term(0, e) - terms[e] - more[e] for e in range(2)]
    finish(2)
    plane_wait(("s", 1), s1)
    terms = above(s1, 3)
    for e in range(2):
        sol[0, e] = (rest[e] - terms[e]).astype(BF16)
    publish(0, None)
    finish(1)

    for sem, ref in sent:
        pltpu.make_async_copy(ref, ref, send_sem.at[sem]).wait()

    for i in range(3):
        wait_moved(send_sem.at[spread_sems[i]], i)

    finish(0)
    for copy in stores:
        copy.wait()


def per_device(right_sides, lower_diag_inverse, upper_diag_inverse, lower_blocks, upper_blocks, block_mask):
    def vmem(*shape):
        return pltpu.VMEM(shape, BF16)

    anywhere = pl.BlockSpec(memory_space=pl.ANY)
    return pl.pallas_call(
        kernel,
        out_shape=jax.ShapeDtypeStruct(right_sides.shape, BF16),
        in_specs=[anywhere] * 5 + [pl.BlockSpec(memory_space=pltpu.SMEM)],
        out_specs=anywhere,
        scratch_shapes=[
            vmem(LEV, B, B),
            vmem(LEV, B, B),
            vmem(2, LEV, B, B),
            vmem(NPAIR, 4, B, B),
            vmem(NPAIR, 4, B, B),
            vmem(LEV, B, B),
            vmem(2, LEV, W, B),
            vmem(2, W, B),
            vmem(CHIPS, 2, W, B),
            vmem(2, 3, 4, B, B),
            vmem(3, NZ, 2, W, B),
            vmem(3, NZ, 2, W, B),
            vmem(3, 4, B, B),
            vmem(3, 2, B, B),
            vmem(3, 2, B, B),
            vmem(3, CHIPS, 2, W, B),
            vmem(3, 2, W, B),
            vmem(3, CHIPS, 2, W, B),
            vmem(NPAIR, B, B),
            vmem(NZ, NPAIR, 32, B),
            vmem(NPAIR, 32, B),
            vmem(2, NZ, 1, 32, B),
            vmem(2, NZ, 2, 32, B),
            vmem(2, NZ, 3, 32, B),
            vmem(LEV, 2, W, B),
            vmem(3, 2, W, B),
            vmem(32, W, B),
            vmem(32, W, B),
            vmem(32, W, B),
            vmem(LEV, 2, W, B),
            vmem(32, W, B),
            vmem(32, W, B),
            vmem(32, W, B),
            vmem(LEV, 16, W, B),
            vmem(LEV, B, B),
            pltpu.SemaphoreType.DMA((16,)),
            pltpu.SemaphoreType.DMA((48,)),
            pltpu.SemaphoreType.DMA((48,)),
        ],
        compiler_params=pltpu.CompilerParams(
            collective_id=0, has_side_effects=True, vmem_limit_bytes=48 * 2**20
        ),
        name="tree_solve",
    )(right_sides, lower_diag_inverse, upper_diag_inverse, lower_blocks, upper_blocks, block_mask)


def solution(mesh):
    in_specs = (
        P(None, "prow", None, None),
        P(None, "prow", None, None),
        P(None, "prow", None, None),
        P(None, "prow", "pcol", None, None),
        P(None, "prow", "pcol", None, None),
        P(),
    )
    return jax.shard_map(
        per_device, mesh=mesh, in_specs=in_specs, out_specs=P(None, "prow", None, None), check_vma=False
    )
```

```python
import functools

import jax
import jax.numpy as jnp
from jax import lax
from jax.experimental import pallas as pl
from jax.experimental.pallas import tpu as pltpu
from jax.sharding import PartitionSpec as P

MESH = pl.DeviceIdType.MESH
F32 = jnp.float32
BF16 = jnp.bfloat16
B = 256
LEV = 4
NPAIR = 6
CHIPS = 16
NZ = 8
W = 16
FIRST = (0, 1, 3)
MOVED = (2, 5, 4)
UORD = (5, 2, 4, 0, 1, 3)
UROW = (2, 1, 1, 0, 0, 0)
ROW_OF = (1, 2, 2, 3, 3, 3)
UGROUPS = ((0, 1), (1, 3), (3, 6))


def dot_nt(a, b):
    return lax.dot_general(a, b, (((1,), (1,)), ((), ())), preferred_element_type=F32)


def kernel(
    rhs_hbm, linv_hbm, uinv_hbm, lower_hbm, upper_hbm, mask,
    out_hbm,
    rhs, linv, uinv, lower, upper,
    g_all, g_home, home, x0, first_m, part, zsum,
    mov, mov_sib, comb, rs_buf, piece, lact,
    ucand, ur_buf0, ur_buf1, upiece, uact0, uact1, uact2,
    fv, u_src, u21, u32, u31,
    sol, s3, s2, s1, out_buf, out_t,
    load_sem, send_sem, recv_sem,
):
    row = lax.axis_index("prow")
    z = lax.axis_index("pcol")
    q = row // 2
    core = row % 2
    other = 1 - core

    def dev(chip, c, zz):
        return (chip * 2 + c, zz)

    sibling = dev(q, other, z)

    loads = {}
    n_load = [0]

    def load(name, src, dst):
        copy = pltpu.make_async_copy(src, dst, load_sem.at[n_load[0]])
        n_load[0] += 1
        copy.start()
        loads[name] = copy

    load("linv", linv_hbm.at[:, 0], linv)
    load("rhs", rhs_hbm.at[:, 0], rhs)
    for p in (2, 0, 5, 4, 1, 3):
        load(("l", p), lower_hbm.at[p, 0], lower.at[p])
    load("uinv", uinv_hbm.at[:, 0], uinv.at[core])
    load("upper", upper_hbm.at[:, 0], upper)

    plane = q // 2
    x, y, qb = q // 4, q % 4, q % 2
    turn = (z - plane + 9) % 8
    flag = 1 - turn // 4
    hx = (x + 3 + 2 * (1 - flag) - turn + 8) % 4
    hy = (y + flag * (2 * qb - 1) + 4) % 4
    home_chip = hx * 4 + hy
    dx = (x - z // 2 + 4) % 4
    dy = (y - 2 * (z % 2) + 4) % 4
    src_qb = ((dy + 1) % 4) // 2
    src_v = 1 - dy // 2
    src_turn = 4 * src_v + (3 + 2 * src_v - dx + 4) % 4
    src_z = (src_turn + 7 + z) % 8
    src_chip = 2 * z + src_qb
    slot = src_qb * 8 + src_z

    barrier = pltpu.get_barrier_semaphore()

    def greet(device):
        pl.semaphore_signal(barrier, inc=1, device_id=device, device_id_type=MESH)

    def greet_plane(d, _):
        greet(dev((q + d) % CHIPS, core, z))
        return 0

    def greet_z(d, _):
        greet(dev(q, core, (z + d) % NZ))
        return 0

    def greet_cross(d, _):
        greet(dev(q, other, (z + d) % NZ))
        return 0

    def greet_move(d, _):
        greet(dev(8 * core + (q + d) % 8, q % 2, q // 2))
        return 0

    own_move = jnp.logical_and(jnp.logical_and(z == q // 2, core == q % 2), core == q // 8)
    lax.fori_loop(1, 8, greet_move, 0)

    @pl.when(jnp.logical_not(own_move))
    def _():
        greet_move(0, 0)

    greet(dev(src_chip, core, src_z))
    greet(dev(src_chip, other, src_z))
    lax.fori_loop(0, NZ, greet_cross, 0)
    lax.fori_loop(1, CHIPS, greet_plane, 0)
    lax.fori_loop(1, NZ, greet_z, 0)

    sent = []

    def remote(src, dst, sem, device):
        pltpu.make_async_remote_copy(
            src_ref=src, dst_ref=dst, send_sem=send_sem.at[sem], recv_sem=recv_sem.at[sem],
            device_id=device, device_id_type=MESH,
        ).start()

    def wait_recv(sem, ref):
        pltpu.make_async_copy(ref, ref, recv_sem.at[sem]).wait()

    sems = {}

    def new_sem(name):
        sems[name] = len(sems)
        return sems[name]

    def to_sibling(name, src, dst):
        sem = new_sem(name)
        remote(src, dst, sem, sibling)
        sent.append((sem, src))

    def plane_gather(name, src, buf, at):
        sem = new_sem(name)

        def body(d, _):
            remote(src, buf.at[at], sem, dev((q + d) % CHIPS, core, z))
            return 0

        lax.fori_loop(1, CHIPS, body, 0)
        buf[at] = src[...]
        sent.append((sem, buf.at[pl.ds(0, 15)] if len(buf.shape) == 4 else buf.at[pl.ds(0, 30)]))

    def plane_wait(name, buf):
        wait_recv(sems[name], buf.at[pl.ds(0, 15)] if len(buf.shape) == 4 else buf.at[pl.ds(0, 30)])

    def z_exchange(name, src_of, buf, at):
        sem = new_sem(name)

        def body(d, _):
            zz = (z + d) % NZ
            remote(src_of(zz), buf.at[at], sem, dev(q, core, zz))
            return 0

        lax.fori_loop(1, NZ, body, 0)
        sent.append((sem, buf.at[pl.ds(0, 7)]))

    loads["linv"].wait()
    loads["rhs"].wait()

    def make_g(h):
        g_all[h] = jnp.dot(linv[h], rhs[h], preferred_element_type=F32).T.astype(BF16)

    def make_m(p, dst, first):
        if first:
            loads[("l", p)].wait()
        for k in range(4):
            weight = mask[p, row, 4 * z + k].astype(F32)
            dst[k] = (jnp.dot(linv[ROW_OF[p]], lower[p, k], preferred_element_type=F32) * weight).astype(BF16)

    def compress_upper(n):
        p = UORD[n]
        found = jnp.int32(0)
        at = jnp.int32(0)
        for k in range(4):
            bit = mask[p, 4 * z + k, row]
            found = found + bit
            at = at + k * bit
        block = jnp.dot(uinv[core, UROW[n]], upper[p, at], preferred_element_type=F32) * found.astype(F32)
        ucand[n] = block.astype(BF16)

    def move_to_sibling(i):
        to_sibling(("mov", i), mov.at[i, pl.ds(2 * other, 2)], mov_sib.at[i])

    def combine(i):
        wait_recv(sems[("mov", i)], mov_sib.at[i])
        for e in range(2):
            comb[i, e] = mov[i, 2 * core + e] + mov_sib[i, e]
        sem = new_sem(("rs", i))

        def body(d, _):
            chip = (q + d) % CHIPS
            rows = pl.ds(pl.multiple_of(chip * W, W), W)
            remote(comb.at[i, :, rows], rs_buf.at[i, q], sem, dev(chip, core, z))
            return 0

        lax.fori_loop(1, CHIPS, body, 0)
        rs_buf[i, q] = comb[i, :, pl.ds(pl.multiple_of(q * W, W), W)]
        sent.append((sem, rs_buf.at[i, pl.ds(0, 15)]))

    def spread(i):
        wait_recv(sems[("rs", i)], rs_buf.at[i, pl.ds(0, 15)])
        total = rs_buf[i, 0].astype(F32)
        for s in range(1, CHIPS):
            total = total + rs_buf[i, s].astype(F32)
        piece[i] = total.astype(BF16)
        sem = new_sem(("lact", i))
        chip = 2 * z + core

        def body(d, _):
            remote(piece.at[i], lact.at[i, q // 8, q % 8], sem, dev(chip, q // 8, (z + d) % NZ))
            return 0

        lax.fori_loop(1, NZ, body, 0)

        @pl.when(own_move)
        def _():
            lact[i, q // 8, q % 8] = piece[i]

        @pl.when(jnp.logical_not(own_move))
        def _():
            body(0, 0)

        return sem

    def wait_moved(sem_ref, i):
        @pl.when(own_move)
        def _():
            ref = lact.at[i, 0, pl.ds(0, 7)]
            pltpu.make_async_copy(ref, ref, sem_ref).wait()

        @pl.when(jnp.logical_not(own_move))
        def _():
            ref = lact.at[i, 0]
            pltpu.make_async_copy(ref, ref, sem_ref).wait()

    spread_sems = {}

    def pass_moved(i):
        wait_moved(recv_sem.at[spread_sems[i]], i)
        to_sibling(("ls", i), lact.at[i, core], lact.at[i, core])

    def moved_ready(i):
        wait_recv(sems[("ls", i)], lact.at[i, 0])

    def products(i):
        wait_recv(sems[("m", i)], first_m.at[0, 0])
        for e in range(2):
            total = None
            for k in range(4):
                cols = x0[8 * (k // 2):8 * (k // 2) + 8, k % 2].reshape(128, B)
                term = dot_nt(cols, first_m[e, i, k])
                total = term if total is None else total + term
            part[i, :, e] = total.astype(BF16).reshape(NZ, W, B)

    def send_products(i):
        z_exchange(("z", i), lambda zz: part.at[i, zz], zsum.at[i], z)
        zsum[i, z] = part[i, z]

    def z_total(i):
        wait_recv(sems[("z", i)], zsum.at[i, pl.ds(0, 7)])
        total = zsum[i, 0].astype(F32)
        for s in range(1, NZ):
            total = total + zsum[i, s].astype(F32)
        return total

    def pushed(buf, p):
        def body(t, carry):
            for j in [t * 8 + u for u in range(8)]:
                val = buf[j].astype(F32)
                carry = tuple(carry[e] + val * mask[p, 2 * q + e, j].astype(F32) for e in range(2))
            return carry

        zero = jnp.zeros((W, B), F32)
        return lax.fori_loop(0, 4, body, (zero, zero))

    def push(name, level, i, slot_, buf):
        for e in range(2):
            block = lact[i, :, :, e].reshape(B, B)
            u_src[slot_, e] = dot_nt(fv[level, e], block).astype(BF16)
        plane_gather(name, u_src.at[slot_], buf, pl.ds(2 * q, 2))

    ur_bufs = (ur_buf0, ur_buf1)

    def reduce_upper(half):
        sem = new_sem(("ur", half))
        buf = ur_bufs[half]

        def body(d, _):
            zz = (z + d) % NZ
            rows = pl.ds(pl.multiple_of(zz * 32, 32), 32)
            remote(ucand.at[pl.ds(3 * half, 3), rows], buf.at[z], sem, dev(q, core, zz))
            return 0

        lax.fori_loop(1, NZ, body, 0)
        buf[z] = ucand[3 * half:3 * half + 3, pl.ds(pl.multiple_of(z * 32, 32), 32)]
        sent.append((sem, buf.at[pl.ds(0, 7)]))

    def total_upper(half):
        buf = ur_bufs[half]
        wait_recv(sems[("ur", half)], buf.at[pl.ds(0, 7)])
        total = buf[0].astype(F32)
        for s in range(1, NZ):
            total = total + buf[s].astype(F32)
        upiece[3 * half:3 * half + 3] = total.astype(BF16)

    uacts = (uact0, uact1, uact2)

    def spread_upper(n):
        lo, hi = UGROUPS[n]
        uact = uacts[n]
        sem = new_sem(("ua", n))

        def body(d, _):
            remote(upiece.at[pl.ds(lo, hi - lo)], uact.at[core, z], sem, dev(q, core, (z + d) % NZ))
            return 0

        lax.fori_loop(1, NZ, body, 0)
        uact[core, z] = upiece[lo:hi]
        sent.append((sem, uact.at[0, pl.ds(0, 7)]))

    def pass_upper(n):
        wait_recv(sems[("ua", n)], uacts[n].at[0, pl.ds(0, 7)])
        to_sibling(("us", n), uacts[n].at[core], uacts[n].at[core])

    def upper_ready(n):
        wait_recv(sems[("us", n)], uacts[n].at[0])

    make_g(0)
    make_m(2, mov.at[0], True)
    make_m(0, first_m.at[core, 0], True)
    for h in range(1, LEV):
        make_g(h)
    loads["uinv"].wait()
    loads["upper"].wait()
    for n in range(NPAIR):
        compress_upper(n)
    pl.semaphore_wait(barrier, 40 - own_move.astype(jnp.int32))

    sem = new_sem("home")
    mine = pl.ds(pl.multiple_of(core * 128 + z * W, W), W)
    yours = pl.ds(pl.multiple_of(other * 128 + z * W, W), W)
    remote(g_all.at[0, mine], home.at[core], sem, dev(home_chip, core, plane))
    remote(g_all.at[0, yours], home.at[core], sem, dev(home_chip, other, plane))
    sent.append((sem, home))
    move_to_sibling(0)
    to_sibling(("m", 0), first_m.at[core, 0], first_m.at[core, 0])
    to_sibling("g", g_all.at[:, yours], g_home.at[core])
    reduce_upper(0)
    g_home[core] = g_all[:, mine]
    for i in (1, 2):
        make_m(MOVED[i], mov.at[i], True)
        move_to_sibling(i)
    combine(0)

    wait_recv(sems["home"], home)
    plane_gather("x0", home, x0, slot)
    reduce_upper(1)
    to_sibling("uinv", uinv.at[core], uinv.at[core])
    for i in (1, 2):
        make_m(FIRST[i], first_m.at[core, i], True)
        to_sibling(("m", i), first_m.at[core, i], first_m.at[core, i])
    spread_sems[0] = spread(0)
    plane_wait("x0", x0)
    products(0)
    send_products(0)
    combine(1)
    combine(2)
    products(1)
    products(2)
    total_upper(0)
    pass_moved(0)
    wait_recv(sems["g"], g_home.at[0])
    for e in range(2):
        fv[0, e] = g_home[e, 0]
    moved_ready(0)
    base = z_total(0)

    for e in range(2):
        fv[1, e] = (g_home[e, 1].astype(F32) - base[e]).astype(BF16)
    push("u21", 1, 0, 0, u21)
    spread_sems[1] = spread(1)
    send_products(1)
    spread_sems[2] = spread(2)
    base = g_home[:, 2].astype(F32) - z_total(1)
    plane_wait("u21", u21)
    low, high = pushed(u21, 2)
    fv[2, 0] = (base[0] - low).astype(BF16)
    fv[2, 1] = (base[1] - high).astype(BF16)
    pass_moved(1)
    moved_ready(1)
    push("u32", 2, 1, 2, u32)
    send_products(2)
    spread_upper(0)
    pass_moved(2)
    moved_ready(2)
    push("u31", 1, 2, 1, u31)
    total_upper(1)
    spread_upper(1)
    base = g_home[:, 3].astype(F32) - z_total(2)
    plane_wait("u32", u32)
    low, high = pushed(u32, 5)
    plane_wait("u31", u31)
    low1, high1 = pushed(u31, 4)
    fv[3, 0] = (base[0] - low1 - low).astype(BF16)
    fv[3, 1] = (base[1] - high1 - high).astype(BF16)

    wait_recv(sems["uinv"], uinv.at[0])

    def own_term(level, e):
        return dot_nt(fv[level, e], uinv[e, level])

    def above(buf, n):
        group = sum(n >= lo for lo, _ in UGROUPS) - 1
        p = UORD[n]

        def body(t, chosen):
            for j in [t * 8 + u for u in range(8)]:
                val = buf[j].astype(F32)
                chosen = tuple(jnp.where(mask[p, j, 2 * q + e] == 1, val, chosen[e]) for e in range(2))
            return chosen

        zero = jnp.zeros((W, B), F32)
        chosen = lax.fori_loop(0, 4, body, (zero, zero))
        blocks = [uacts[group][e, :, n - UGROUPS[group][0]].reshape(B, B) for e in range(2)]
        return [dot_nt(chosen[e].astype(BF16), blocks[e]) for e in range(2)]

    def gather_level(level, buf):
        plane_gather(("s", level), sol.at[level], buf, pl.ds(2 * q, 2))

    def publish(level):
        sem = new_sem(("out", level))
        at = core * 8 + z

        def body(d, _):
            remote(sol.at[level, core], out_buf.at[level, at], sem, dev(q, core, (z + d) % NZ))
            return 0

        def cross(d, _):
            remote(sol.at[level, other], out_buf.at[level, at], sem, dev(q, other, (z + d) % NZ))
            return 0

        lax.fori_loop(1, NZ, body, 0)
        lax.fori_loop(0, NZ, cross, 0)
        out_buf[level, at] = sol[level, core]
        sent.append((sem, out_buf.at[level, pl.ds(0, 15)]))

    stores = []

    def finish(level):
        wait_recv(sems[("out", level)], out_buf.at[level, pl.ds(0, 15)])
        out_t[level] = out_buf[level].reshape(B, B).astype(F32).T.astype(BF16)
        copy = pltpu.make_async_copy(out_t.at[level], out_hbm.at[level, 0], load_sem.at[n_load[0]])
        n_load[0] += 1
        copy.start()
        stores.append(copy)

    for e in range(2):
        sol[3, e] = own_term(3, e).astype(BF16)
    gather_level(3, s3)
    spread_upper(2)
    rest = [own_term(2, e) for e in range(2)]
    pass_upper(0)
    upper_ready(0)
    plane_wait(("s", 3), s3)
    terms = above(s3, 0)
    for e in range(2):
        sol[2, e] = (rest[e] - terms[e]).astype(BF16)
    gather_level(2, s2)
    publish(3)
    pass_upper(1)
    upper_ready(1)
    terms = above(s3, 2)
    rest = [own_term(1, e) - terms[e] for e in range(2)]
    plane_wait(("s", 2), s2)
    terms = above(s2, 1)
    for e in range(2):
        sol[1, e] = (rest[e] - terms[e]).astype(BF16)
    gather_level(1, s1)
    publish(2)
    publish(1)
    pass_upper(2)
    upper_ready(2)
    terms = above(s3, 5)
    more = above(s2, 4)
    rest = [own_term(0, e) - terms[e] - more[e] for e in range(2)]
    finish(3)
    plane_wait(("s", 1), s1)
    terms = above(s1, 3)
    for e in range(2):
        sol[0, e] = (rest[e] - terms[e]).astype(BF16)
    publish(0)
    finish(2)
    finish(1)

    for sem, ref in sent:
        pltpu.make_async_copy(ref, ref, send_sem.at[sem]).wait()

    for i in range(3):
        wait_moved(send_sem.at[spread_sems[i]], i)

    finish(0)
    for copy in stores:
        copy.wait()


def per_device(right_sides, lower_diag_inverse, upper_diag_inverse, lower_blocks, upper_blocks, block_mask):
    def vmem(*shape):
        return pltpu.VMEM(shape, BF16)

    anywhere = pl.BlockSpec(memory_space=pl.ANY)
    hbm = pl.BlockSpec(memory_space=pltpu.HBM)
    return pl.pallas_call(
        kernel,
        out_shape=jax.ShapeDtypeStruct(right_sides.shape, BF16),
        in_specs=[hbm] * 5 + [pl.BlockSpec(memory_space=pltpu.SMEM)],
        out_specs=anywhere,
        scratch_shapes=[
            vmem(LEV, B, B),
            vmem(LEV, B, B),
            vmem(2, LEV, B, B),
            vmem(NPAIR, 4, B, B),
            vmem(NPAIR, 4, B, B),
            vmem(LEV, B, B),
            vmem(2, LEV, W, B),
            vmem(2, W, B),
            vmem(CHIPS, 2, W, B),
            vmem(2, 3, 4, B, B),
            vmem(3, NZ, 2, W, B),
            vmem(3, NZ, 2, W, B),
            vmem(3, 4, B, B),
            vmem(3, 2, B, B),
            vmem(3, 2, B, B),
            vmem(3, CHIPS, 2, W, B),
            vmem(3, 2, W, B),
            vmem(3, 2, 8, 2, W, B),
            vmem(NPAIR, B, B),
            vmem(NZ, 3, 32, B),
            vmem(NZ, 3, 32, B),
            vmem(NPAIR, 32, B),
            vmem(2, NZ, 1, 32, B),
            vmem(2, NZ, 2, 32, B),
            vmem(2, NZ, 3, 32, B),
            vmem(LEV, 2, W, B),
            vmem(3, 2, W, B),
            vmem(32, W, B),
            vmem(32, W, B),
            vmem(32, W, B),
            vmem(LEV, 2, W, B),
            vmem(32, W, B),
            vmem(32, W, B),
            vmem(32, W, B),
            vmem(LEV, 16, W, B),
            vmem(LEV, B, B),
            pltpu.SemaphoreType.DMA((16,)),
            pltpu.SemaphoreType.DMA((48,)),
            pltpu.SemaphoreType.DMA((48,)),
        ],
        compiler_params=pltpu.CompilerParams(
            collective_id=0, has_side_effects=True, vmem_limit_bytes=63 * 2**20
        ),
        name="tree_solve",
    )(right_sides, lower_diag_inverse, upper_diag_inverse, lower_blocks, upper_blocks, block_mask)


def solution(mesh):
    in_specs = (
        P(None, "prow", None, None),
        P(None, "prow", None, None),
        P(None, "prow", None, None),
        P(None, "prow", "pcol", None, None),
        P(None, "prow", "pcol", None, None),
        P(),
    )
    return jax.shard_map(
        per_device, mesh=mesh, in_specs=in_specs, out_specs=P(None, "prow", None, None), check_vma=False
    )
```

```python
import functools

import jax
import jax.numpy as jnp
from jax import lax
from jax.experimental import pallas as pl
from jax.experimental.pallas import tpu as pltpu
from jax.sharding import PartitionSpec as P

MESH = pl.DeviceIdType.MESH
F32 = jnp.float32
BF16 = jnp.bfloat16
B = 256
LEV = 4
NPAIR = 6
CHIPS = 16
NZ = 8
W = 16
FIRST = (0, 1, 3)
MOVED = (2, 5, 4)
UORD = (5, 2, 4, 0, 1, 3)
UROW = (2, 1, 1, 0, 0, 0)
ROW_OF = (1, 2, 2, 3, 3, 3)
UGROUPS = ((0, 1), (1, 3), (3, 6))
UHALVES = ((0, 4), (4, 6))


def dot_nt(a, b):
    return lax.dot_general(a, b, (((1,), (1,)), ((), ())), preferred_element_type=F32)


def kernel(
    rhs_hbm, linv_hbm, uinv_hbm, lower_hbm, upper_hbm, mask,
    out_hbm,
    rhs, linv, uinv, lower, upper,
    g_all, g_home, home, x0, first_m, part, zsum,
    mov, mov_sib, comb, rs_buf, piece, lact,
    ucand, ur_buf0, ur_buf1, upiece, uact0, uact1, uact2,
    fv, u_src, u21, u32, u31,
    sol, s3, s2, s1, out_buf, out_t,
    load_sem, send_sem, recv_sem,
):
    row = lax.axis_index("prow")
    z = lax.axis_index("pcol")
    q = row // 2
    core = row % 2
    other = 1 - core

    def dev(chip, c, zz):
        return (chip * 2 + c, zz)

    sibling = dev(q, other, z)

    loads = {}
    n_load = [0]

    def load(name, src, dst):
        copy = pltpu.make_async_copy(src, dst, load_sem.at[n_load[0]])
        n_load[0] += 1
        copy.start()
        loads[name] = copy

    load("linv", linv_hbm.at[:, 0], linv)
    load("rhs", rhs_hbm.at[:, 0], rhs)
    for p in (2, 0, 5, 4, 1, 3):
        load(("l", p), lower_hbm.at[p, 0], lower.at[p])
    load("uinv", uinv_hbm.at[:, 0], uinv.at[core])
    load("upper", upper_hbm.at[:, 0], upper)

    plane = q // 2
    x, y, qb = q // 4, q % 4, q % 2
    turn = (z - plane + 9) % 8
    flag = 1 - turn // 4
    hx = (x + 3 + 2 * (1 - flag) - turn + 8) % 4
    hy = (y + flag * (2 * qb - 1) + 4) % 4
    home_chip = hx * 4 + hy
    dx = (x - z // 2 + 4) % 4
    dy = (y - 2 * (z % 2) + 4) % 4
    src_qb = ((dy + 1) % 4) // 2
    src_v = 1 - dy // 2
    src_turn = 4 * src_v + (3 + 2 * src_v - dx + 4) % 4
    src_z = (src_turn + 7 + z) % 8
    src_chip = 2 * z + src_qb
    slot = src_qb * 8 + src_z

    barrier = pltpu.get_barrier_semaphore()

    def greet(device):
        pl.semaphore_signal(barrier, inc=1, device_id=device, device_id_type=MESH)

    def greet_plane(d, _):
        greet(dev((q + d) % CHIPS, core, z))
        return 0

    def greet_z(d, _):
        greet(dev(q, core, (z + d) % NZ))
        return 0

    def greet_cross(d, _):
        greet(dev(q, other, (z + d) % NZ))
        return 0

    def greet_move(d, _):
        greet(dev(8 * core + (q + d) % 8, q % 2, q // 2))
        return 0

    own_move = jnp.logical_and(jnp.logical_and(z == q // 2, core == q % 2), core == q // 8)
    lax.fori_loop(1, 8, greet_move, 0)

    @pl.when(jnp.logical_not(own_move))
    def _():
        greet_move(0, 0)

    greet(dev(src_chip, core, src_z))
    greet(dev(src_chip, other, src_z))
    lax.fori_loop(0, NZ, greet_cross, 0)
    lax.fori_loop(1, CHIPS, greet_plane, 0)
    lax.fori_loop(1, NZ, greet_z, 0)

    sent = []

    def remote(src, dst, sem, device):
        pltpu.make_async_remote_copy(
            src_ref=src, dst_ref=dst, send_sem=send_sem.at[sem], recv_sem=recv_sem.at[sem],
            device_id=device, device_id_type=MESH,
        ).start()

    def wait_recv(sem, ref):
        pltpu.make_async_copy(ref, ref, recv_sem.at[sem]).wait()

    sems = {}

    def new_sem(name):
        sems[name] = len(sems)
        return sems[name]

    def to_sibling(name, src, dst):
        sem = new_sem(name)
        remote(src, dst, sem, sibling)
        sent.append((sem, src))

    def plane_gather(name, src, buf, at):
        sem = new_sem(name)

        def body(d, _):
            remote(src, buf.at[at], sem, dev((q + d) % CHIPS, core, z))
            return 0

        lax.fori_loop(1, CHIPS, body, 0)
        buf[at] = src[...]
        sent.append((sem, buf.at[pl.ds(0, 15)] if len(buf.shape) == 4 else buf.at[pl.ds(0, 30)]))

    def plane_wait(name, buf):
        wait_recv(sems[name], buf.at[pl.ds(0, 15)] if len(buf.shape) == 4 else buf.at[pl.ds(0, 30)])

    def z_exchange(name, src_of, buf, at):
        sem = new_sem(name)

        def body(d, _):
            zz = (z + d) % NZ
            remote(src_of(zz), buf.at[at], sem, dev(q, core, zz))
            return 0

        lax.fori_loop(1, NZ, body, 0)
        sent.append((sem, buf.at[pl.ds(0, 7)]))

    loads["linv"].wait()
    loads["rhs"].wait()

    def make_g(h):
        g_all[h] = jnp.dot(linv[h], rhs[h], preferred_element_type=F32).T.astype(BF16)

    def make_m(p, dst, first):
        if first:
            loads[("l", p)].wait()
        for k in range(4):
            weight = mask[p, row, 4 * z + k].astype(F32)
            dst[k] = (jnp.dot(linv[ROW_OF[p]], lower[p, k], preferred_element_type=F32) * weight).astype(BF16)

    def compress_upper(n):
        p = UORD[n]
        found = jnp.int32(0)
        at = jnp.int32(0)
        for k in range(4):
            bit = mask[p, 4 * z + k, row]
            found = found + bit
            at = at + k * bit
        block = jnp.dot(uinv[core, UROW[n]], upper[p, at], preferred_element_type=F32) * found.astype(F32)
        ucand[n] = block.astype(BF16)

    def move_to_sibling(i):
        to_sibling(("mov", i), mov.at[i, pl.ds(2 * other, 2)], mov_sib.at[i])

    def combine(i):
        wait_recv(sems[("mov", i)], mov_sib.at[i])
        for e in range(2):
            comb[i, e] = mov[i, 2 * core + e] + mov_sib[i, e]
        sem = new_sem(("rs", i))

        def body(d, _):
            chip = (q + d) % CHIPS
            rows = pl.ds(pl.multiple_of(chip * W, W), W)
            remote(comb.at[i, :, rows], rs_buf.at[i, q], sem, dev(chip, core, z))
            return 0

        lax.fori_loop(1, CHIPS, body, 0)
        rs_buf[i, q] = comb[i, :, pl.ds(pl.multiple_of(q * W, W), W)]
        sent.append((sem, rs_buf.at[i, pl.ds(0, 15)]))

    def spread(i):
        wait_recv(sems[("rs", i)], rs_buf.at[i, pl.ds(0, 15)])
        total = rs_buf[i, 0].astype(F32)
        for s in range(1, CHIPS):
            total = total + rs_buf[i, s].astype(F32)
        piece[i] = total.astype(BF16)
        sem = new_sem(("lact", i))
        chip = 2 * z + core

        def body(d, _):
            remote(piece.at[i], lact.at[i, q // 8, q % 8], sem, dev(chip, q // 8, (z + d) % NZ))
            return 0

        lax.fori_loop(1, NZ, body, 0)

        @pl.when(own_move)
        def _():
            lact[i, q // 8, q % 8] = piece[i]

        @pl.when(jnp.logical_not(own_move))
        def _():
            body(0, 0)

        return sem

    def wait_moved(sem_ref, i):
        @pl.when(own_move)
        def _():
            ref = lact.at[i, 0, pl.ds(0, 7)]
            pltpu.make_async_copy(ref, ref, sem_ref).wait()

        @pl.when(jnp.logical_not(own_move))
        def _():
            ref = lact.at[i, 0]
            pltpu.make_async_copy(ref, ref, sem_ref).wait()

    spread_sems = {}

    def pass_moved(i):
        wait_moved(recv_sem.at[spread_sems[i]], i)
        to_sibling(("ls", i), lact.at[i, core], lact.at[i, core])

    def moved_ready(i):
        wait_recv(sems[("ls", i)], lact.at[i, 0])

    def products(i):
        wait_recv(sems[("m", i)], first_m.at[0, 0])
        for e in range(2):
            total = None
            for k in range(4):
                cols = x0[8 * (k // 2):8 * (k // 2) + 8, k % 2].reshape(128, B)
                term = dot_nt(cols, first_m[e, i, k])
                total = term if total is None else total + term
            part[i, :, e] = total.astype(BF16).reshape(NZ, W, B)

    def send_products(i):
        z_exchange(("z", i), lambda zz: part.at[i, zz], zsum.at[i], z)
        zsum[i, z] = part[i, z]

    def z_total(i):
        wait_recv(sems[("z", i)], zsum.at[i, pl.ds(0, 7)])
        total = zsum[i, 0].astype(F32)
        for s in range(1, NZ):
            total = total + zsum[i, s].astype(F32)
        return total

    def pushed(buf, p):
        def body(t, carry):
            for j in [t * 8 + u for u in range(8)]:
                val = buf[j].astype(F32)
                carry = tuple(carry[e] + val * mask[p, 2 * q + e, j].astype(F32) for e in range(2))
            return carry

        zero = jnp.zeros((W, B), F32)
        return lax.fori_loop(0, 4, body, (zero, zero))

    def push(name, level, i, slot_, buf):
        for e in range(2):
            block = lact[i, :, :, e].reshape(B, B)
            u_src[slot_, e] = dot_nt(fv[level, e], block).astype(BF16)
        plane_gather(name, u_src.at[slot_], buf, pl.ds(2 * q, 2))

    ur_bufs = (ur_buf0, ur_buf1)

    def reduce_upper(half):
        lo, hi = UHALVES[half]
        sem = new_sem(("ur", half))
        buf = ur_bufs[half]

        def body(d, _):
            zz = (z + d) % NZ
            rows = pl.ds(pl.multiple_of(zz * 32, 32), 32)
            remote(ucand.at[pl.ds(lo, hi - lo), rows], buf.at[z], sem, dev(q, core, zz))
            return 0

        lax.fori_loop(1, NZ, body, 0)
        buf[z] = ucand[lo:hi, pl.ds(pl.multiple_of(z * 32, 32), 32)]
        sent.append((sem, buf.at[pl.ds(0, 7)]))

    def total_upper(half):
        lo, hi = UHALVES[half]
        buf = ur_bufs[half]
        wait_recv(sems[("ur", half)], buf.at[pl.ds(0, 7)])
        total = buf[0].astype(F32)
        for s in range(1, NZ):
            total = total + buf[s].astype(F32)
        upiece[lo:hi] = total.astype(BF16)

    uacts = (uact0, uact1, uact2)

    def spread_upper(n):
        lo, hi = UGROUPS[n]
        uact = uacts[n]
        sem = new_sem(("ua", n))

        def body(d, _):
            remote(upiece.at[pl.ds(lo, hi - lo)], uact.at[core, z], sem, dev(q, core, (z + d) % NZ))
            return 0

        lax.fori_loop(1, NZ, body, 0)
        uact[core, z] = upiece[lo:hi]
        sent.append((sem, uact.at[0, pl.ds(0, 7)]))

    def pass_upper(n):
        wait_recv(sems[("ua", n)], uacts[n].at[0, pl.ds(0, 7)])
        to_sibling(("us", n), uacts[n].at[core], uacts[n].at[core])

    def upper_ready(n):
        wait_recv(sems[("us", n)], uacts[n].at[0])

    make_g(0)
    make_m(2, mov.at[0], True)
    make_m(0, first_m.at[core, 0], True)
    for h in range(1, LEV):
        make_g(h)
    loads["uinv"].wait()
    loads["upper"].wait()
    for n in range(NPAIR):
        compress_upper(n)
    pl.semaphore_wait(barrier, 40 - own_move.astype(jnp.int32))

    sem = new_sem("home")
    mine = pl.ds(pl.multiple_of(core * 128 + z * W, W), W)
    yours = pl.ds(pl.multiple_of(other * 128 + z * W, W), W)
    remote(g_all.at[0, mine], home.at[core], sem, dev(home_chip, core, plane))
    remote(g_all.at[0, yours], home.at[core], sem, dev(home_chip, other, plane))
    sent.append((sem, home))
    move_to_sibling(0)
    to_sibling(("m", 0), first_m.at[core, 0], first_m.at[core, 0])
    to_sibling("g", g_all.at[:, yours], g_home.at[core])
    reduce_upper(0)
    g_home[core] = g_all[:, mine]
    for i in (1, 2):
        make_m(MOVED[i], mov.at[i], True)
        move_to_sibling(i)
    combine(0)
    combine(1)

    wait_recv(sems["home"], home)
    plane_gather("x0", home, x0, slot)
    to_sibling("uinv", uinv.at[core], uinv.at[core])
    for i in (1, 2):
        make_m(FIRST[i], first_m.at[core, i], True)
        to_sibling(("m", i), first_m.at[core, i], first_m.at[core, i])
    spread_sems[0] = spread(0)
    plane_wait("x0", x0)
    products(0)
    send_products(0)
    combine(2)
    products(1)
    send_products(1)
    spread_sems[1] = spread(1)
    products(2)
    total_upper(0)
    pass_moved(0)
    wait_recv(sems["g"], g_home.at[0])
    for e in range(2):
        fv[0, e] = g_home[e, 0]
    moved_ready(0)
    base = z_total(0)

    for e in range(2):
        fv[1, e] = (g_home[e, 1].astype(F32) - base[e]).astype(BF16)
    push("u21", 1, 0, 0, u21)
    spread_sems[2] = spread(2)
    send_products(2)
    reduce_upper(1)
    base = g_home[:, 2].astype(F32) - z_total(1)
    plane_wait("u21", u21)
    low, high = pushed(u21, 2)
    fv[2, 0] = (base[0] - low).astype(BF16)
    fv[2, 1] = (base[1] - high).astype(BF16)
    pass_moved(1)
    moved_ready(1)
    push("u32", 2, 1, 2, u32)
    spread_upper(0)
    spread_upper(1)
    pass_moved(2)
    moved_ready(2)
    push("u31", 1, 2, 1, u31)
    base = g_home[:, 3].astype(F32) - z_total(2)
    plane_wait("u32", u32)
    low, high = pushed(u32, 5)
    plane_wait("u31", u31)
    low1, high1 = pushed(u31, 4)
    fv[3, 0] = (base[0] - low1 - low).astype(BF16)
    fv[3, 1] = (base[1] - high1 - high).astype(BF16)

    wait_recv(sems["uinv"], uinv.at[0])

    def own_term(level, e):
        return dot_nt(fv[level, e], uinv[e, level])

    def above(buf, n):
        group = sum(n >= lo for lo, _ in UGROUPS) - 1
        p = UORD[n]

        def body(t, chosen):
            for j in [t * 8 + u for u in range(8)]:
                val = buf[j].astype(F32)
                chosen = tuple(jnp.where(mask[p, j, 2 * q + e] == 1, val, chosen[e]) for e in range(2))
            return chosen

        zero = jnp.zeros((W, B), F32)
        chosen = lax.fori_loop(0, 4, body, (zero, zero))
        blocks = [uacts[group][e, :, n - UGROUPS[group][0]].reshape(B, B) for e in range(2)]
        return [dot_nt(chosen[e].astype(BF16), blocks[e]) for e in range(2)]

    def gather_level(level, buf):
        plane_gather(("s", level), sol.at[level], buf, pl.ds(2 * q, 2))

    def publish(level):
        sem = new_sem(("out", level))
        at = core * 8 + z

        def body(d, _):
            remote(sol.at[level, core], out_buf.at[level, at], sem, dev(q, core, (z + d) % NZ))
            return 0

        def cross(d, _):
            remote(sol.at[level, other], out_buf.at[level, at], sem, dev(q, other, (z + d) % NZ))
            return 0

        lax.fori_loop(1, NZ, body, 0)
        lax.fori_loop(0, NZ, cross, 0)
        out_buf[level, at] = sol[level, core]
        sent.append((sem, out_buf.at[level, pl.ds(0, 15)]))

    stores = []

    def finish(level):
        wait_recv(sems[("out", level)], out_buf.at[level, pl.ds(0, 15)])
        out_t[level] = out_buf[level].reshape(B, B).astype(F32).T.astype(BF16)
        copy = pltpu.make_async_copy(out_t.at[level], out_hbm.at[level, 0], load_sem.at[n_load[0]])
        n_load[0] += 1
        copy.start()
        stores.append(copy)

    for e in range(2):
        sol[3, e] = own_term(3, e).astype(BF16)
    gather_level(3, s3)
    total_upper(1)
    spread_upper(2)
    rest = [own_term(2, e) for e in range(2)]
    pass_upper(0)
    upper_ready(0)
    plane_wait(("s", 3), s3)
    terms = above(s3, 0)
    for e in range(2):
        sol[2, e] = (rest[e] - terms[e]).astype(BF16)
    gather_level(2, s2)
    pass_upper(1)
    upper_ready(1)
    publish(3)
    terms = above(s3, 2)
    rest = [own_term(1, e) - terms[e] for e in range(2)]
    plane_wait(("s", 2), s2)
    terms = above(s2, 1)
    for e in range(2):
        sol[1, e] = (rest[e] - terms[e]).astype(BF16)
    gather_level(1, s1)
    publish(2)
    pass_upper(2)
    publish(1)
    upper_ready(2)
    terms = above(s3, 5)
    more = above(s2, 4)
    rest = [own_term(0, e) - terms[e] - more[e] for e in range(2)]
    plane_wait(("s", 1), s1)
    terms = above(s1, 3)
    for e in range(2):
        sol[0, e] = (rest[e] - terms[e]).astype(BF16)
    publish(0)
    finish(3)
    finish(2)
    finish(1)

    for sem, ref in sent:
        pltpu.make_async_copy(ref, ref, send_sem.at[sem]).wait()

    for i in range(3):
        wait_moved(send_sem.at[spread_sems[i]], i)

    finish(0)
    for copy in stores:
        copy.wait()


def per_device(right_sides, lower_diag_inverse, upper_diag_inverse, lower_blocks, upper_blocks, block_mask):
    def vmem(*shape):
        return pltpu.VMEM(shape, BF16)

    anywhere = pl.BlockSpec(memory_space=pl.ANY)
    hbm = pl.BlockSpec(memory_space=pltpu.HBM)
    return pl.pallas_call(
        kernel,
        out_shape=jax.ShapeDtypeStruct(right_sides.shape, BF16),
        in_specs=[hbm] * 5 + [pl.BlockSpec(memory_space=pltpu.SMEM)],
        out_specs=anywhere,
        scratch_shapes=[
            vmem(LEV, B, B),
            vmem(LEV, B, B),
            vmem(2, LEV, B, B),
            vmem(NPAIR, 4, B, B),
            vmem(NPAIR, 4, B, B),
            vmem(LEV, B, B),
            vmem(2, LEV, W, B),
            vmem(2, W, B),
            vmem(CHIPS, 2, W, B),
            vmem(2, 3, 4, B, B),
            vmem(3, NZ, 2, W, B),
            vmem(3, NZ, 2, W, B),
            vmem(3, 4, B, B),
            vmem(3, 2, B, B),
            vmem(3, 2, B, B),
            vmem(3, CHIPS, 2, W, B),
            vmem(3, 2, W, B),
            vmem(3, 2, 8, 2, W, B),
            vmem(NPAIR, B, B),
            vmem(NZ, 4, 32, B),
            vmem(NZ, 2, 32, B),
            vmem(NPAIR, 32, B),
            vmem(2, NZ, 1, 32, B),
            vmem(2, NZ, 2, 32, B),
            vmem(2, NZ, 3, 32, B),
            vmem(LEV, 2, W, B),
            vmem(3, 2, W, B),
            vmem(32, W, B),
            vmem(32, W, B),
            vmem(32, W, B),
            vmem(LEV, 2, W, B),
            vmem(32, W, B),
            vmem(32, W, B),
            vmem(32, W, B),
            vmem(LEV, 16, W, B),
            vmem(LEV, B, B),
            pltpu.SemaphoreType.DMA((16,)),
            pltpu.SemaphoreType.DMA((48,)),
            pltpu.SemaphoreType.DMA((48,)),
        ],
        compiler_params=pltpu.CompilerParams(
            collective_id=0, has_side_effects=True, vmem_limit_bytes=63 * 2**20
        ),
        name="tree_solve",
    )(right_sides, lower_diag_inverse, upper_diag_inverse, lower_blocks, upper_blocks, block_mask)


def solution(mesh):
    in_specs = (
        P(None, "prow", None, None),
        P(None, "prow", None, None),
        P(None, "prow", None, None),
        P(None, "prow", "pcol", None, None),
        P(None, "prow", "pcol", None, None),
        P(),
    )
    return jax.shard_map(
        per_device, mesh=mesh, in_specs=in_specs, out_specs=P(None, "prow", None, None), check_vma=False
    )
```

```python
import functools

import jax
import jax.numpy as jnp
from jax import lax
from jax.experimental import pallas as pl
from jax.experimental.pallas import tpu as pltpu
from jax.sharding import PartitionSpec as P

MESH = pl.DeviceIdType.MESH
F32 = jnp.float32
BF16 = jnp.bfloat16
B = 256
LEV = 4
NPAIR = 6
CHIPS = 16
NZ = 8
W = 16
FIRST = (0, 1, 3)
MOVED = (2, 5, 4)
UORD = (5, 2, 4, 0, 1, 3)
UROW = (2, 1, 1, 0, 0, 0)
ROW_OF = (1, 2, 2, 3, 3, 3)
UGROUPS = ((0, 1), (1, 3), (3, 6))


def dot_nt(a, b):
    return lax.dot_general(a, b, (((1,), (1,)), ((), ())), preferred_element_type=F32)


def kernel(
    rhs_hbm, linv_hbm, uinv_hbm, lower_hbm, upper_hbm, mask,
    out_hbm,
    rhs, linv, uinv, lower, upper,
    g_all, g_home, home, x0, first_m, part, zsum,
    mov, mov_sib, comb, rs_buf, piece, lact,
    ucand, ring_r, ring_l, sum_r, sum_l, upiece, uact0, uact1, uact2,
    fv, u_src, u21, u32, u31,
    sol, s3, s2, s1, out_buf, out_t,
    load_sem, send_sem, recv_sem,
):
    row = lax.axis_index("prow")
    z = lax.axis_index("pcol")
    q = row // 2
    core = row % 2
    other = 1 - core

    def dev(chip, c, zz):
        return (chip * 2 + c, zz)

    sibling = dev(q, other, z)

    loads = {}
    n_load = [0]

    def load(name, src, dst):
        copy = pltpu.make_async_copy(src, dst, load_sem.at[n_load[0]])
        n_load[0] += 1
        copy.start()
        loads[name] = copy

    load("linv", linv_hbm.at[:, 0], linv)
    load("rhs", rhs_hbm.at[:, 0], rhs)
    for p in (2, 0, 5, 4, 1, 3):
        load(("l", p), lower_hbm.at[p, 0], lower.at[p])
    load("uinv", uinv_hbm.at[:, 0], uinv.at[core])
    load("upper", upper_hbm.at[:, 0], upper)

    plane = q // 2
    x, y, qb = q // 4, q % 4, q % 2
    turn = (z - plane + 9) % 8
    flag = 1 - turn // 4
    hx = (x + 3 + 2 * (1 - flag) - turn + 8) % 4
    hy = (y + flag * (2 * qb - 1) + 4) % 4
    home_chip = hx * 4 + hy
    dx = (x - z // 2 + 4) % 4
    dy = (y - 2 * (z % 2) + 4) % 4
    src_qb = ((dy + 1) % 4) // 2
    src_v = 1 - dy // 2
    src_turn = 4 * src_v + (3 + 2 * src_v - dx + 4) % 4
    src_z = (src_turn + 7 + z) % 8
    src_chip = 2 * z + src_qb
    slot = src_qb * 8 + src_z

    barrier = pltpu.get_barrier_semaphore()

    def greet(device):
        pl.semaphore_signal(barrier, inc=1, device_id=device, device_id_type=MESH)

    def greet_plane(d, _):
        greet(dev((q + d) % CHIPS, core, z))
        return 0

    def greet_z(d, _):
        greet(dev(q, core, (z + d) % NZ))
        return 0

    def greet_cross(d, _):
        greet(dev(q, other, (z + d) % NZ))
        return 0

    def greet_move(d, _):
        greet(dev(8 * core + (q + d) % 8, q % 2, q // 2))
        return 0

    own_move = jnp.logical_and(jnp.logical_and(z == q // 2, core == q % 2), core == q // 8)
    lax.fori_loop(1, 8, greet_move, 0)

    @pl.when(jnp.logical_not(own_move))
    def _():
        greet_move(0, 0)

    greet(dev(src_chip, core, src_z))
    greet(dev(src_chip, other, src_z))
    lax.fori_loop(0, NZ, greet_cross, 0)
    lax.fori_loop(1, CHIPS, greet_plane, 0)
    lax.fori_loop(1, NZ, greet_z, 0)

    sent = []

    def remote(src, dst, sem, device):
        pltpu.make_async_remote_copy(
            src_ref=src, dst_ref=dst, send_sem=send_sem.at[sem], recv_sem=recv_sem.at[sem],
            device_id=device, device_id_type=MESH,
        ).start()

    def wait_recv(sem, ref):
        pltpu.make_async_copy(ref, ref, recv_sem.at[sem]).wait()

    sems = {}

    def new_sem(name):
        sems[name] = len(sems)
        return sems[name]

    def to_sibling(name, src, dst):
        sem = new_sem(name)
        remote(src, dst, sem, sibling)
        sent.append((sem, src))

    def plane_gather(name, src, buf, at):
        sem = new_sem(name)

        def body(d, _):
            remote(src, buf.at[at], sem, dev((q + d) % CHIPS, core, z))
            return 0

        lax.fori_loop(1, CHIPS, body, 0)
        buf[at] = src[...]
        sent.append((sem, buf.at[pl.ds(0, 15)] if len(buf.shape) == 4 else buf.at[pl.ds(0, 30)]))

    def plane_wait(name, buf):
        wait_recv(sems[name], buf.at[pl.ds(0, 15)] if len(buf.shape) == 4 else buf.at[pl.ds(0, 30)])

    def z_exchange(name, src_of, buf, at):
        sem = new_sem(name)

        def body(d, _):
            zz = (z + d) % NZ
            remote(src_of(zz), buf.at[at], sem, dev(q, core, zz))
            return 0

        lax.fori_loop(1, NZ, body, 0)
        sent.append((sem, buf.at[pl.ds(0, 7)]))

    loads["linv"].wait()
    loads["rhs"].wait()

    def make_g(h):
        g_all[h] = jnp.dot(linv[h], rhs[h], preferred_element_type=F32).T.astype(BF16)

    def make_m(p, dst, first):
        if first:
            loads[("l", p)].wait()
        for k in range(4):
            weight = mask[p, row, 4 * z + k].astype(F32)
            dst[k] = (jnp.dot(linv[ROW_OF[p]], lower[p, k], preferred_element_type=F32) * weight).astype(BF16)

    def compress_upper(n):
        p = UORD[n]
        found = jnp.int32(0)
        at = jnp.int32(0)
        for k in range(4):
            bit = mask[p, 4 * z + k, row]
            found = found + bit
            at = at + k * bit
        block = jnp.dot(uinv[core, UROW[n]], upper[p, at], preferred_element_type=F32) * found.astype(F32)
        ucand[n] = block.astype(BF16)

    def move_to_sibling(i):
        to_sibling(("mov", i), mov.at[i, pl.ds(2 * other, 2)], mov_sib.at[i])

    def combine(i):
        wait_recv(sems[("mov", i)], mov_sib.at[i])
        for e in range(2):
            comb[i, e] = mov[i, 2 * core + e] + mov_sib[i, e]
        sem = new_sem(("rs", i))

        def body(d, _):
            chip = (q + d) % CHIPS
            rows = pl.ds(pl.multiple_of(chip * W, W), W)
            remote(comb.at[i, :, rows], rs_buf.at[i, q], sem, dev(chip, core, z))
            return 0

        lax.fori_loop(1, CHIPS, body, 0)
        rs_buf[i, q] = comb[i, :, pl.ds(pl.multiple_of(q * W, W), W)]
        sent.append((sem, rs_buf.at[i, pl.ds(0, 15)]))

    def spread(i):
        wait_recv(sems[("rs", i)], rs_buf.at[i, pl.ds(0, 15)])
        total = rs_buf[i, 0].astype(F32)
        for s in range(1, CHIPS):
            total = total + rs_buf[i, s].astype(F32)
        piece[i] = total.astype(BF16)
        sem = new_sem(("lact", i))
        chip = 2 * z + core

        def body(d, _):
            remote(piece.at[i], lact.at[i, q // 8, q % 8], sem, dev(chip, q // 8, (z + d) % NZ))
            return 0

        lax.fori_loop(1, NZ, body, 0)

        @pl.when(own_move)
        def _():
            lact[i, q // 8, q % 8] = piece[i]

        @pl.when(jnp.logical_not(own_move))
        def _():
            body(0, 0)

        return sem

    def wait_moved(sem_ref, i):
        @pl.when(own_move)
        def _():
            ref = lact.at[i, 0, pl.ds(0, 7)]
            pltpu.make_async_copy(ref, ref, sem_ref).wait()

        @pl.when(jnp.logical_not(own_move))
        def _():
            ref = lact.at[i, 0]
            pltpu.make_async_copy(ref, ref, sem_ref).wait()

    spread_sems = {}

    def pass_moved(i):
        wait_moved(recv_sem.at[spread_sems[i]], i)
        to_sibling(("ls", i), lact.at[i, core], lact.at[i, core])

    def moved_ready(i):
        wait_recv(sems[("ls", i)], lact.at[i, 0])

    def products(i):
        wait_recv(sems[("m", i)], first_m.at[0, 0])
        for e in range(2):
            total = None
            for k in range(4):
                cols = x0[8 * (k // 2):8 * (k // 2) + 8, k % 2].reshape(128, B)
                term = dot_nt(cols, first_m[e, i, k])
                total = term if total is None else total + term
            part[i, :, e] = total.astype(BF16).reshape(NZ, W, B)

    def send_products(i):
        z_exchange(("z", i), lambda zz: part.at[i, zz], zsum.at[i], z)
        zsum[i, z] = part[i, z]

    def z_total(i):
        wait_recv(sems[("z", i)], zsum.at[i, pl.ds(0, 7)])
        total = zsum[i, 0].astype(F32)
        for s in range(1, NZ):
            total = total + zsum[i, s].astype(F32)
        return total

    def pushed(buf, p):
        def body(t, carry):
            for j in [t * 8 + u for u in range(8)]:
                val = buf[j].astype(F32)
                carry = tuple(carry[e] + val * mask[p, 2 * q + e, j].astype(F32) for e in range(2))
            return carry

        zero = jnp.zeros((W, B), F32)
        return lax.fori_loop(0, 4, body, (zero, zero))

    def push(name, level, i, slot_, buf):
        for e in range(2):
            block = lact[i, :, :, e].reshape(B, B)
            u_src[slot_, e] = dot_nt(fv[level, e], block).astype(BF16)
        plane_gather(name, u_src.at[slot_], buf, pl.ds(2 * q, 2))

    def upper_rows(shift):
        return pl.ds(pl.multiple_of((z + NZ + shift) % NZ * 32, 32), 32)

    def ring_send(way, n, src):
        sem = new_sem(("ring", way, n))
        buf = (ring_r if way > 0 else ring_l).at[n]
        remote(src, buf, sem, dev(q, core, (z + NZ + way) % NZ))
        sent.append((sem, buf))

    def ring_start():
        ring_send(1, 0, ucand.at[:, upper_rows(4)])
        ring_send(-1, 0, ucand.at[:, upper_rows(-3)])

    def ring_step(n):
        wait_recv(sems[("ring", 1, n - 1)], ring_r.at[n - 1])
        sum_r[n - 1] = ring_r[n - 1] + ucand[:, upper_rows(4 - n)]
        ring_send(1, n, sum_r.at[n - 1])
        if n < 3:
            wait_recv(sems[("ring", -1, n - 1)], ring_l.at[n - 1])
            sum_l[n - 1] = ring_l[n - 1] + ucand[:, upper_rows(n - 3)]
            ring_send(-1, n, sum_l.at[n - 1])

    def ring_end():
        wait_recv(sems[("ring", 1, 3)], ring_r.at[3])
        wait_recv(sems[("ring", -1, 2)], ring_l.at[2])
        upiece[...] = ring_r[3] + ring_l[2] + ucand[:, upper_rows(0)]

    uacts = (uact0, uact1, uact2)

    def spread_upper(n):
        lo, hi = UGROUPS[n]
        uact = uacts[n]
        sem = new_sem(("ua", n))

        def body(d, _):
            remote(upiece.at[pl.ds(lo, hi - lo)], uact.at[core, z], sem, dev(q, core, (z + d) % NZ))
            return 0

        lax.fori_loop(1, NZ, body, 0)
        uact[core, z] = upiece[lo:hi]
        sent.append((sem, uact.at[0, pl.ds(0, 7)]))

    def pass_upper(n):
        wait_recv(sems[("ua", n)], uacts[n].at[0, pl.ds(0, 7)])
        to_sibling(("us", n), uacts[n].at[core], uacts[n].at[core])

    def upper_ready(n):
        wait_recv(sems[("us", n)], uacts[n].at[0])

    make_g(0)
    make_m(2, mov.at[0], True)
    make_m(0, first_m.at[core, 0], True)
    for h in range(1, LEV):
        make_g(h)
    loads["uinv"].wait()
    loads["upper"].wait()
    for n in range(NPAIR):
        compress_upper(n)
    pl.semaphore_wait(barrier, 40 - own_move.astype(jnp.int32))

    sem = new_sem("home")
    mine = pl.ds(pl.multiple_of(core * 128 + z * W, W), W)
    yours = pl.ds(pl.multiple_of(other * 128 + z * W, W), W)
    remote(g_all.at[0, mine], home.at[core], sem, dev(home_chip, core, plane))
    remote(g_all.at[0, yours], home.at[core], sem, dev(home_chip, other, plane))
    sent.append((sem, home))
    move_to_sibling(0)
    to_sibling(("m", 0), first_m.at[core, 0], first_m.at[core, 0])
    to_sibling("g", g_all.at[:, yours], g_home.at[core])
    ring_start()
    g_home[core] = g_all[:, mine]
    for i in (1, 2):
        make_m(MOVED[i], mov.at[i], True)
        move_to_sibling(i)
    combine(0)
    combine(1)

    wait_recv(sems["home"], home)
    plane_gather("x0", home, x0, slot)
    to_sibling("uinv", uinv.at[core], uinv.at[core])
    combine(2)
    ring_step(1)
    for i in (1, 2):
        make_m(FIRST[i], first_m.at[core, i], True)
        to_sibling(("m", i), first_m.at[core, i], first_m.at[core, i])
    spread_sems[0] = spread(0)
    ring_step(2)
    spread_sems[1] = spread(1)
    plane_wait("x0", x0)
    products(0)
    send_products(0)
    ring_step(3)
    spread_sems[2] = spread(2)
    products(1)
    send_products(1)
    products(2)
    pass_moved(0)
    wait_recv(sems["g"], g_home.at[0])
    for e in range(2):
        fv[0, e] = g_home[e, 0]
    moved_ready(0)
    base = z_total(0)

    for e in range(2):
        fv[1, e] = (g_home[e, 1].astype(F32) - base[e]).astype(BF16)
    push("u21", 1, 0, 0, u21)
    send_products(2)
    pass_moved(1)
    pass_moved(2)
    ring_end()
    spread_upper(0)
    base = g_home[:, 2].astype(F32) - z_total(1)
    plane_wait("u21", u21)
    low, high = pushed(u21, 2)
    fv[2, 0] = (base[0] - low).astype(BF16)
    fv[2, 1] = (base[1] - high).astype(BF16)
    moved_ready(1)
    push("u32", 2, 1, 2, u32)
    moved_ready(2)
    push("u31", 1, 2, 1, u31)
    for n in (1, 2):
        spread_upper(n)
    base = g_home[:, 3].astype(F32) - z_total(2)
    plane_wait("u32", u32)
    low, high = pushed(u32, 5)
    plane_wait("u31", u31)
    low1, high1 = pushed(u31, 4)
    fv[3, 0] = (base[0] - low1 - low).astype(BF16)
    fv[3, 1] = (base[1] - high1 - high).astype(BF16)

    wait_recv(sems["uinv"], uinv.at[0])

    def own_term(level, e):
        return dot_nt(fv[level, e], uinv[e, level])

    def above(buf, n):
        group = sum(n >= lo for lo, _ in UGROUPS) - 1
        p = UORD[n]

        def body(t, chosen):
            for j in [t * 8 + u for u in range(8)]:
                val = buf[j].astype(F32)
                chosen = tuple(jnp.where(mask[p, j, 2 * q + e] == 1, val, chosen[e]) for e in range(2))
            return chosen

        zero = jnp.zeros((W, B), F32)
        chosen = lax.fori_loop(0, 4, body, (zero, zero))
        blocks = [uacts[group][e, :, n - UGROUPS[group][0]].reshape(B, B) for e in range(2)]
        return [dot_nt(chosen[e].astype(BF16), blocks[e]) for e in range(2)]

    def gather_level(level, buf):
        plane_gather(("s", level), sol.at[level], buf, pl.ds(2 * q, 2))

    def publish(level):
        sem = new_sem(("out", level))
        at = core * 8 + z

        def body(d, _):
            remote(sol.at[level, core], out_buf.at[level, at], sem, dev(q, core, (z + d) % NZ))
            return 0

        def cross(d, _):
            remote(sol.at[level, other], out_buf.at[level, at], sem, dev(q, other, (z + d) % NZ))
            return 0

        lax.fori_loop(1, NZ, body, 0)
        lax.fori_loop(0, NZ, cross, 0)
        out_buf[level, at] = sol[level, core]
        sent.append((sem, out_buf.at[level, pl.ds(0, 15)]))

    stores = []

    def finish(level):
        wait_recv(sems[("out", level)], out_buf.at[level, pl.ds(0, 15)])
        out_t[level] = out_buf[level].reshape(B, B).astype(F32).T.astype(BF16)
        copy = pltpu.make_async_copy(out_t.at[level], out_hbm.at[level, 0], load_sem.at[n_load[0]])
        n_load[0] += 1
        copy.start()
        stores.append(copy)

    for e in range(2):
        sol[3, e] = own_term(3, e).astype(BF16)
    gather_level(3, s3)
    rest = [own_term(2, e) for e in range(2)]
    pass_upper(0)
    upper_ready(0)
    plane_wait(("s", 3), s3)
    terms = above(s3, 0)
    for e in range(2):
        sol[2, e] = (rest[e] - terms[e]).astype(BF16)
    gather_level(2, s2)
    pass_upper(1)
    upper_ready(1)
    publish(3)
    terms = above(s3, 2)
    rest = [own_term(1, e) - terms[e] for e in range(2)]
    plane_wait(("s", 2), s2)
    terms = above(s2, 1)
    for e in range(2):
        sol[1, e] = (rest[e] - terms[e]).astype(BF16)
    gather_level(1, s1)
    publish(2)
    pass_upper(2)
    publish(1)
    upper_ready(2)
    terms = above(s3, 5)
    more = above(s2, 4)
    rest = [own_term(0, e) - terms[e] - more[e] for e in range(2)]
    plane_wait(("s", 1), s1)
    terms = above(s1, 3)
    for e in range(2):
        sol[0, e] = (rest[e] - terms[e]).astype(BF16)
    publish(0)
    finish(3)
    finish(2)
    finish(1)

    for sem, ref in sent:
        pltpu.make_async_copy(ref, ref, send_sem.at[sem]).wait()

    for i in range(3):
        wait_moved(send_sem.at[spread_sems[i]], i)

    finish(0)
    for copy in stores:
        copy.wait()


def per_device(right_sides, lower_diag_inverse, upper_diag_inverse, lower_blocks, upper_blocks, block_mask):
    def vmem(*shape):
        return pltpu.VMEM(shape, BF16)

    anywhere = pl.BlockSpec(memory_space=pl.ANY)
    hbm = pl.BlockSpec(memory_space=pltpu.HBM)
    return pl.pallas_call(
        kernel,
        out_shape=jax.ShapeDtypeStruct(right_sides.shape, BF16),
        in_specs=[hbm] * 5 + [pl.BlockSpec(memory_space=pltpu.SMEM)],
        out_specs=anywhere,
        scratch_shapes=[
            vmem(LEV, B, B),
            vmem(LEV, B, B),
            vmem(2, LEV, B, B),
            vmem(NPAIR, 4, B, B),
            vmem(NPAIR, 4, B, B),
            vmem(LEV, B, B),
            vmem(2, LEV, W, B),
            vmem(2, W, B),
            vmem(CHIPS, 2, W, B),
            vmem(2, 3, 4, B, B),
            vmem(3, NZ, 2, W, B),
            vmem(3, NZ, 2, W, B),
            vmem(3, 4, B, B),
            vmem(3, 2, B, B),
            vmem(3, 2, B, B),
            vmem(3, CHIPS, 2, W, B),
            vmem(3, 2, W, B),
            vmem(3, 2, 8, 2, W, B),
            vmem(NPAIR, B, B),
            vmem(4, NPAIR, 32, B),
            vmem(3, NPAIR, 32, B),
            vmem(3, NPAIR, 32, B),
            vmem(2, NPAIR, 32, B),
            vmem(NPAIR, 32, B),
            vmem(2, NZ, 1, 32, B),
            vmem(2, NZ, 2, 32, B),
            vmem(2, NZ, 3, 32, B),
            vmem(LEV, 2, W, B),
            vmem(3, 2, W, B),
            vmem(32, W, B),
            vmem(32, W, B),
            vmem(32, W, B),
            vmem(LEV, 2, W, B),
            vmem(32, W, B),
            vmem(32, W, B),
            vmem(32, W, B),
            vmem(LEV, 16, W, B),
            vmem(LEV, B, B),
            pltpu.SemaphoreType.DMA((16,)),
            pltpu.SemaphoreType.DMA((48,)),
            pltpu.SemaphoreType.DMA((48,)),
        ],
        compiler_params=pltpu.CompilerParams(
            collective_id=0, has_side_effects=True, vmem_limit_bytes=63 * 2**20
        ),
        name="tree_solve",
    )(right_sides, lower_diag_inverse, upper_diag_inverse, lower_blocks, upper_blocks, block_mask)


def solution(mesh):
    in_specs = (
        P(None, "prow", None, None),
        P(None, "prow", None, None),
        P(None, "prow", None, None),
        P(None, "prow", "pcol", None, None),
        P(None, "prow", "pcol", None, None),
        P(),
    )
    return jax.shard_map(
        per_device, mesh=mesh, in_specs=in_specs, out_specs=P(None, "prow", None, None), check_vma=False
    )
```

```python
import functools

import jax
import jax.numpy as jnp
from jax import lax
from jax.experimental import pallas as pl
from jax.experimental.pallas import tpu as pltpu
from jax.sharding import PartitionSpec as P

MESH = pl.DeviceIdType.MESH
F32 = jnp.float32
BF16 = jnp.bfloat16
B = 256
LEV = 4
NPAIR = 6
CHIPS = 16
NZ = 8
W = 16
FIRST = (0, 1, 3)
MOVED = (2, 5, 4)
UORD = (5, 2, 4, 0, 1, 3)
UROW = (2, 1, 1, 0, 0, 0)
ROW_OF = (1, 2, 2, 3, 3, 3)
UGROUPS = ((0, 1), (1, 3), (3, 6))


def dot_nt(a, b):
    return lax.dot_general(a, b, (((1,), (1,)), ((), ())), preferred_element_type=F32)


def kernel(
    rhs_hbm, linv_hbm, uinv_hbm, lower_hbm, upper_hbm, mask,
    out_hbm,
    rhs, linv, uinv, lower, upper,
    g_all, g_home, home, x0, first_m, part, zsum,
    mov, mov_sib, comb, rs_buf, piece, lact,
    ucand, ring_r, ring_l, sum_r, sum_l, upiece, uact0, uact1, uact2,
    fv, u_src, u21, u32, u31,
    sol, s3, s2, s1, out_buf, out_t,
    load_sem, send_sem, recv_sem,
):
    row = lax.axis_index("prow")
    z = lax.axis_index("pcol")
    q = row // 2
    core = row % 2
    other = 1 - core

    def dev(chip, c, zz):
        return (chip * 2 + c, zz)

    sibling = dev(q, other, z)

    loads = {}
    n_load = [0]

    def load(name, src, dst):
        copy = pltpu.make_async_copy(src, dst, load_sem.at[n_load[0]])
        n_load[0] += 1
        copy.start()
        loads[name] = copy

    load("linv", linv_hbm.at[:, 0], linv)
    load("rhs", rhs_hbm.at[:, 0], rhs)
    for p in (2, 0, 5, 4, 1, 3):
        load(("l", p), lower_hbm.at[p, 0], lower.at[p])
    load("uinv", uinv_hbm.at[:, 0], uinv.at[core])
    load("upper", upper_hbm.at[:, 0], upper)

    plane = q // 2
    x, y, qb = q // 4, q % 4, q % 2
    turn = (z - plane + 9) % 8
    flag = 1 - turn // 4
    hx = (x + 3 + 2 * (1 - flag) - turn + 8) % 4
    hy = (y + flag * (2 * qb - 1) + 4) % 4
    home_chip = hx * 4 + hy
    dx = (x - z // 2 + 4) % 4
    dy = (y - 2 * (z % 2) + 4) % 4
    src_qb = ((dy + 1) % 4) // 2
    src_v = 1 - dy // 2
    src_turn = 4 * src_v + (3 + 2 * src_v - dx + 4) % 4
    src_z = (src_turn + 7 + z) % 8
    src_chip = 2 * z + src_qb
    slot = src_qb * 8 + src_z

    barrier = pltpu.get_barrier_semaphore()

    def greet(device):
        pl.semaphore_signal(barrier, inc=1, device_id=device, device_id_type=MESH)

    def greet_plane(d, _):
        greet(dev((q + d) % CHIPS, core, z))
        return 0

    def greet_z(d, _):
        greet(dev(q, core, (z + d) % NZ))
        return 0

    def greet_cross(d, _):
        greet(dev(q, other, (z + d) % NZ))
        return 0

    def greet_move(d, _):
        greet(dev(8 * core + (q + d) % 8, q % 2, q // 2))
        return 0

    own_move = jnp.logical_and(jnp.logical_and(z == q // 2, core == q % 2), core == q // 8)
    lax.fori_loop(1, 8, greet_move, 0)

    @pl.when(jnp.logical_not(own_move))
    def _():
        greet_move(0, 0)

    greet(dev(src_chip, core, src_z))
    greet(dev(src_chip, other, src_z))
    lax.fori_loop(0, NZ, greet_cross, 0)
    lax.fori_loop(1, CHIPS, greet_plane, 0)
    lax.fori_loop(1, NZ, greet_z, 0)

    sent = []

    def remote(src, dst, sem, device):
        pltpu.make_async_remote_copy(
            src_ref=src, dst_ref=dst, send_sem=send_sem.at[sem], recv_sem=recv_sem.at[sem],
            device_id=device, device_id_type=MESH,
        ).start()

    def wait_recv(sem, ref):
        pltpu.make_async_copy(ref, ref, recv_sem.at[sem]).wait()

    sems = {}

    def new_sem(name):
        sems[name] = len(sems)
        return sems[name]

    def to_sibling(name, src, dst):
        sem = new_sem(name)
        remote(src, dst, sem, sibling)
        sent.append((sem, src))

    def plane_gather(name, src, buf, at):
        sem = new_sem(name)

        def body(d, _):
            remote(src, buf.at[at], sem, dev((q + d) % CHIPS, core, z))
            return 0

        lax.fori_loop(1, CHIPS, body, 0)
        buf[at] = src[...]
        sent.append((sem, buf.at[pl.ds(0, 15)] if len(buf.shape) == 4 else buf.at[pl.ds(0, 30)]))

    def plane_wait(name, buf):
        wait_recv(sems[name], buf.at[pl.ds(0, 15)] if len(buf.shape) == 4 else buf.at[pl.ds(0, 30)])

    def z_exchange(name, src_of, buf, at):
        sem = new_sem(name)

        def body(d, _):
            zz = (z + d) % NZ
            remote(src_of(zz), buf.at[at], sem, dev(q, core, zz))
            return 0

        lax.fori_loop(1, NZ, body, 0)
        sent.append((sem, buf.at[pl.ds(0, 7)]))

    loads["linv"].wait()
    loads["rhs"].wait()

    def make_g(h):
        g_all[h] = jnp.dot(linv[h], rhs[h], preferred_element_type=F32).T.astype(BF16)

    def make_m(p, dst, first):
        if first:
            loads[("l", p)].wait()
        for k in range(4):
            weight = mask[p, row, 4 * z + k].astype(F32)
            dst[k] = (jnp.dot(linv[ROW_OF[p]], lower[p, k], preferred_element_type=F32) * weight).astype(BF16)

    def compress_upper(n):
        p = UORD[n]
        found = jnp.int32(0)
        at = jnp.int32(0)
        for k in range(4):
            bit = mask[p, 4 * z + k, row]
            found = found + bit
            at = at + k * bit
        block = jnp.dot(uinv[core, UROW[n]], upper[p, at], preferred_element_type=F32) * found.astype(F32)
        ucand[n] = block.astype(BF16)

    def move_to_sibling(i):
        to_sibling(("mov", i), mov.at[i, pl.ds(2 * other, 2)], mov_sib.at[i])

    def combine(i):
        wait_recv(sems[("mov", i)], mov_sib.at[i])
        for e in range(2):
            comb[i, e] = mov[i, 2 * core + e] + mov_sib[i, e]
        sem = new_sem(("rs", i))

        def body(d, _):
            chip = (q + d) % CHIPS
            rows = pl.ds(pl.multiple_of(chip * W, W), W)
            remote(comb.at[i, :, rows], rs_buf.at[i, q], sem, dev(chip, core, z))
            return 0

        lax.fori_loop(1, CHIPS, body, 0)
        rs_buf[i, q] = comb[i, :, pl.ds(pl.multiple_of(q * W, W), W)]
        sent.append((sem, rs_buf.at[i, pl.ds(0, 15)]))

    def spread(i):
        wait_recv(sems[("rs", i)], rs_buf.at[i, pl.ds(0, 15)])
        total = rs_buf[i, 0].astype(F32)
        for s in range(1, CHIPS):
            total = total + rs_buf[i, s].astype(F32)
        piece[i] = total.astype(BF16)
        sem = new_sem(("lact", i))
        chip = 2 * z + core

        def body(d, _):
            remote(piece.at[i], lact.at[i, q // 8, q % 8], sem, dev(chip, q // 8, (z + d) % NZ))
            return 0

        lax.fori_loop(1, NZ, body, 0)

        @pl.when(own_move)
        def _():
            lact[i, q // 8, q % 8] = piece[i]

        @pl.when(jnp.logical_not(own_move))
        def _():
            body(0, 0)

        return sem

    def wait_moved(sem_ref, i):
        @pl.when(own_move)
        def _():
            ref = lact.at[i, 0, pl.ds(0, 7)]
            pltpu.make_async_copy(ref, ref, sem_ref).wait()

        @pl.when(jnp.logical_not(own_move))
        def _():
            ref = lact.at[i, 0]
            pltpu.make_async_copy(ref, ref, sem_ref).wait()

    spread_sems = {}

    def pass_moved(i):
        wait_moved(recv_sem.at[spread_sems[i]], i)
        to_sibling(("ls", i), lact.at[i, core], lact.at[i, core])

    def moved_ready(i):
        wait_recv(sems[("ls", i)], lact.at[i, 0])

    def products(i):
        wait_recv(sems[("m", i)], first_m.at[0, 0])
        for e in range(2):
            total = None
            for k in range(4):
                cols = x0[8 * (k // 2):8 * (k // 2) + 8, k % 2].reshape(128, B)
                term = dot_nt(cols, first_m[e, i, k])
                total = term if total is None else total + term
            part[i, :, e] = total.astype(BF16).reshape(NZ, W, B)

    def send_products(i):
        z_exchange(("z", i), lambda zz: part.at[i, zz], zsum.at[i], z)
        zsum[i, z] = part[i, z]

    def z_total(i):
        wait_recv(sems[("z", i)], zsum.at[i, pl.ds(0, 7)])
        total = zsum[i, 0].astype(F32)
        for s in range(1, NZ):
            total = total + zsum[i, s].astype(F32)
        return total

    def pushed(buf, p):
        def body(t, carry):
            for j in [t * 8 + u for u in range(8)]:
                val = buf[j].astype(F32)
                carry = tuple(carry[e] + val * mask[p, 2 * q + e, j].astype(F32) for e in range(2))
            return carry

        zero = jnp.zeros((W, B), F32)
        return lax.fori_loop(0, 4, body, (zero, zero))

    def push(name, level, i, slot_, buf):
        for e in range(2):
            block = lact[i, :, :, e].reshape(B, B)
            u_src[slot_, e] = dot_nt(fv[level, e], block).astype(BF16)
        plane_gather(name, u_src.at[slot_], buf, pl.ds(2 * q, 2))

    def upper_rows(shift):
        return pl.ds(pl.multiple_of((z + NZ + shift) % NZ * 32, 32), 32)

    def ring_send(way, n, src):
        sem = new_sem(("ring", way, n))
        buf = (ring_r if way > 0 else ring_l).at[n]
        remote(src, buf, sem, dev(q, core, (z + NZ + way) % NZ))
        sent.append((sem, buf))

    def ring_start():
        ring_send(1, 0, ucand.at[:, upper_rows(4)])
        ring_send(-1, 0, ucand.at[:, upper_rows(-3)])

    def ring_step(n):
        wait_recv(sems[("ring", 1, n - 1)], ring_r.at[n - 1])
        sum_r[n - 1] = ring_r[n - 1] + ucand[:, upper_rows(4 - n)]
        ring_send(1, n, sum_r.at[n - 1])
        if n < 3:
            wait_recv(sems[("ring", -1, n - 1)], ring_l.at[n - 1])
            sum_l[n - 1] = ring_l[n - 1] + ucand[:, upper_rows(n - 3)]
            ring_send(-1, n, sum_l.at[n - 1])

    def ring_end():
        wait_recv(sems[("ring", 1, 3)], ring_r.at[3])
        wait_recv(sems[("ring", -1, 2)], ring_l.at[2])
        upiece[...] = ring_r[3] + ring_l[2] + ucand[:, upper_rows(0)]

    uacts = (uact0, uact1, uact2)

    def spread_upper(n):
        lo, hi = UGROUPS[n]
        uact = uacts[n]
        sem = new_sem(("ua", n))

        def body(d, _):
            remote(upiece.at[pl.ds(lo, hi - lo)], uact.at[core, z], sem, dev(q, core, (z + d) % NZ))
            return 0

        lax.fori_loop(1, NZ, body, 0)
        uact[core, z] = upiece[lo:hi]
        sent.append((sem, uact.at[0, pl.ds(0, 7)]))

    def pass_upper(n):
        wait_recv(sems[("ua", n)], uacts[n].at[0, pl.ds(0, 7)])
        to_sibling(("us", n), uacts[n].at[core], uacts[n].at[core])

    def upper_ready(n):
        wait_recv(sems[("us", n)], uacts[n].at[0])

    make_g(0)
    make_m(2, mov.at[0], True)
    make_m(0, first_m.at[core, 0], True)
    for h in range(1, LEV):
        make_g(h)
    loads["uinv"].wait()
    loads["upper"].wait()
    for n in range(NPAIR):
        compress_upper(n)
    pl.semaphore_wait(barrier, 40 - own_move.astype(jnp.int32))

    sem = new_sem("home")
    mine = pl.ds(pl.multiple_of(core * 128 + z * W, W), W)
    yours = pl.ds(pl.multiple_of(other * 128 + z * W, W), W)
    remote(g_all.at[0, mine], home.at[core], sem, dev(home_chip, core, plane))
    remote(g_all.at[0, yours], home.at[core], sem, dev(home_chip, other, plane))
    sent.append((sem, home))
    move_to_sibling(0)
    to_sibling(("m", 0), first_m.at[core, 0], first_m.at[core, 0])
    to_sibling("g", g_all.at[:, yours], g_home.at[core])
    ring_start()
    g_home[core] = g_all[:, mine]
    for i in (1, 2):
        make_m(MOVED[i], mov.at[i], True)
        move_to_sibling(i)
    combine(0)

    wait_recv(sems["home"], home)
    plane_gather("x0", home, x0, slot)
    to_sibling("uinv", uinv.at[core], uinv.at[core])
    ring_step(1)
    for i in (1, 2):
        make_m(FIRST[i], first_m.at[core, i], True)
        to_sibling(("m", i), first_m.at[core, i], first_m.at[core, i])
    spread_sems[0] = spread(0)
    ring_step(2)
    plane_wait("x0", x0)
    products(0)
    send_products(0)
    combine(1)
    combine(2)
    ring_step(3)
    products(1)
    send_products(1)
    products(2)
    pass_moved(0)
    wait_recv(sems["g"], g_home.at[0])
    for e in range(2):
        fv[0, e] = g_home[e, 0]
    spread_sems[1] = spread(1)
    moved_ready(0)
    base = z_total(0)

    for e in range(2):
        fv[1, e] = (g_home[e, 1].astype(F32) - base[e]).astype(BF16)
    push("u21", 1, 0, 0, u21)
    spread_sems[2] = spread(2)
    ring_end()
    base = g_home[:, 2].astype(F32) - z_total(1)
    plane_wait("u21", u21)
    low, high = pushed(u21, 2)
    fv[2, 0] = (base[0] - low).astype(BF16)
    fv[2, 1] = (base[1] - high).astype(BF16)
    send_products(2)
    pass_moved(1)
    moved_ready(1)
    push("u32", 2, 1, 2, u32)
    pass_moved(2)
    moved_ready(2)
    push("u31", 1, 2, 1, u31)
    for n in range(3):
        spread_upper(n)
    base = g_home[:, 3].astype(F32) - z_total(2)
    plane_wait("u32", u32)
    low, high = pushed(u32, 5)
    plane_wait("u31", u31)
    low1, high1 = pushed(u31, 4)
    fv[3, 0] = (base[0] - low1 - low).astype(BF16)
    fv[3, 1] = (base[1] - high1 - high).astype(BF16)

    wait_recv(sems["uinv"], uinv.at[0])

    def own_term(level, e):
        return dot_nt(fv[level, e], uinv[e, level])

    def above(buf, n):
        group = sum(n >= lo for lo, _ in UGROUPS) - 1
        p = UORD[n]

        def body(t, chosen):
            for j in [t * 8 + u for u in range(8)]:
                val = buf[j].astype(F32)
                chosen = tuple(jnp.where(mask[p, j, 2 * q + e] == 1, val, chosen[e]) for e in range(2))
            return chosen

        zero = jnp.zeros((W, B), F32)
        chosen = lax.fori_loop(0, 4, body, (zero, zero))
        blocks = [uacts[group][e, :, n - UGROUPS[group][0]].reshape(B, B) for e in range(2)]
        return [dot_nt(chosen[e].astype(BF16), blocks[e]) for e in range(2)]

    def gather_level(level, buf):
        plane_gather(("s", level), sol.at[level], buf, pl.ds(2 * q, 2))

    def publish(level):
        sem = new_sem(("out", level))
        at = core * 8 + z

        def body(d, _):
            remote(sol.at[level, core], out_buf.at[level, at], sem, dev(q, core, (z + d) % NZ))
            return 0

        def cross(d, _):
            remote(sol.at[level, other], out_buf.at[level, at], sem, dev(q, other, (z + d) % NZ))
            return 0

        lax.fori_loop(1, NZ, body, 0)
        lax.fori_loop(0, NZ, cross, 0)
        out_buf[level, at] = sol[level, core]
        sent.append((sem, out_buf.at[level, pl.ds(0, 15)]))

    stores = []

    def finish(level):
        wait_recv(sems[("out", level)], out_buf.at[level, pl.ds(0, 15)])
        out_t[level] = out_buf[level].reshape(B, B).astype(F32).T.astype(BF16)
        copy = pltpu.make_async_copy(out_t.at[level], out_hbm.at[level, 0], load_sem.at[n_load[0]])
        n_load[0] += 1
        copy.start()
        stores.append(copy)

    for e in range(2):
        sol[3, e] = own_term(3, e).astype(BF16)
    gather_level(3, s3)
    rest = [own_term(2, e) for e in range(2)]
    pass_upper(0)
    upper_ready(0)
    plane_wait(("s", 3), s3)
    terms = above(s3, 0)
    for e in range(2):
        sol[2, e] = (rest[e] - terms[e]).astype(BF16)
    gather_level(2, s2)
    pass_upper(1)
    upper_ready(1)
    publish(3)
    terms = above(s3, 2)
    rest = [own_term(1, e) - terms[e] for e in range(2)]
    plane_wait(("s", 2), s2)
    terms = above(s2, 1)
    for e in range(2):
        sol[1, e] = (rest[e] - terms[e]).astype(BF16)
    gather_level(1, s1)
    publish(2)
    pass_upper(2)
    publish(1)
    upper_ready(2)
    terms = above(s3, 5)
    more = above(s2, 4)
    rest = [own_term(0, e) - terms[e] - more[e] for e in range(2)]
    plane_wait(("s", 1), s1)
    terms = above(s1, 3)
    for e in range(2):
        sol[0, e] = (rest[e] - terms[e]).astype(BF16)
    publish(0)
    finish(3)
    finish(2)
    finish(1)

    for sem, ref in sent:
        pltpu.make_async_copy(ref, ref, send_sem.at[sem]).wait()

    for i in range(3):
        wait_moved(send_sem.at[spread_sems[i]], i)

    finish(0)
    for copy in stores:
        copy.wait()


def per_device(right_sides, lower_diag_inverse, upper_diag_inverse, lower_blocks, upper_blocks, block_mask):
    def vmem(*shape):
        return pltpu.VMEM(shape, BF16)

    anywhere = pl.BlockSpec(memory_space=pl.ANY)
    hbm = pl.BlockSpec(memory_space=pltpu.HBM)
    return pl.pallas_call(
        kernel,
        out_shape=jax.ShapeDtypeStruct(right_sides.shape, BF16),
        in_specs=[hbm] * 5 + [pl.BlockSpec(memory_space=pltpu.SMEM)],
        out_specs=anywhere,
        scratch_shapes=[
            vmem(LEV, B, B),
            vmem(LEV, B, B),
            vmem(2, LEV, B, B),
            vmem(NPAIR, 4, B, B),
            vmem(NPAIR, 4, B, B),
            vmem(LEV, B, B),
            vmem(2, LEV, W, B),
            vmem(2, W, B),
            vmem(CHIPS, 2, W, B),
            vmem(2, 3, 4, B, B),
            vmem(3, NZ, 2, W, B),
            vmem(3, NZ, 2, W, B),
            vmem(3, 4, B, B),
            vmem(3, 2, B, B),
            vmem(3, 2, B, B),
            vmem(3, CHIPS, 2, W, B),
            vmem(3, 2, W, B),
            vmem(3, 2, 8, 2, W, B),
            vmem(NPAIR, B, B),
            vmem(4, NPAIR, 32, B),
            vmem(3, NPAIR, 32, B),
            vmem(3, NPAIR, 32, B),
            vmem(2, NPAIR, 32, B),
            vmem(NPAIR, 32, B),
            vmem(2, NZ, 1, 32, B),
            vmem(2, NZ, 2, 32, B),
            vmem(2, NZ, 3, 32, B),
            vmem(LEV, 2, W, B),
            vmem(3, 2, W, B),
            vmem(32, W, B),
            vmem(32, W, B),
            vmem(32, W, B),
            vmem(LEV, 2, W, B),
            vmem(32, W, B),
            vmem(32, W, B),
            vmem(32, W, B),
            vmem(LEV, 16, W, B),
            vmem(LEV, B, B),
            pltpu.SemaphoreType.DMA((16,)),
            pltpu.SemaphoreType.DMA((48,)),
            pltpu.SemaphoreType.DMA((48,)),
        ],
        compiler_params=pltpu.CompilerParams(
            collective_id=0, has_side_effects=True, vmem_limit_bytes=532 * 2**20 // 10
        ),
        name="tree_solve",
    )(right_sides, lower_diag_inverse, upper_diag_inverse, lower_blocks, upper_blocks, block_mask)


def solution(mesh):
    in_specs = (
        P(None, "prow", None, None),
        P(None, "prow", None, None),
        P(None, "prow", None, None),
        P(None, "prow", "pcol", None, None),
        P(None, "prow", "pcol", None, None),
        P(),
    )
    return jax.shard_map(
        per_device, mesh=mesh, in_specs=in_specs, out_specs=P(None, "prow", None, None), check_vma=False
    )
```

```python
import functools

import jax
import jax.numpy as jnp
from jax import lax
from jax.experimental import pallas as pl
from jax.experimental.pallas import tpu as pltpu
from jax.sharding import PartitionSpec as P

MESH = pl.DeviceIdType.MESH
F32 = jnp.float32
BF16 = jnp.bfloat16
B = 256
LEV = 4
NPAIR = 6
CHIPS = 16
NZ = 8
W = 16
FIRST = (0, 1, 3)
MOVED = (2, 5, 4)
UORD = (5, 2, 4, 0, 1, 3)
UROW = (2, 1, 1, 0, 0, 0)
ROW_OF = (1, 2, 2, 3, 3, 3)
UGROUPS = ((0, 1), (1, 3), (3, 6))


def dot_nt(a, b):
    return lax.dot_general(a, b, (((1,), (1,)), ((), ())), preferred_element_type=F32)


def kernel(
    rhs_hbm, linv_hbm, uinv_hbm, lower_hbm, upper_hbm, mask,
    out_hbm,
    rhs, linv, uinv, lower, upper,
    g_all, g_home, home, x0, first_m, part, zsum,
    mov, mov_sib, comb, rs_buf, piece, lact,
    ucand, ring_r, ring_l, sum_r, sum_l, upiece, uact0, uact1, uact2,
    fv, u_src, u21, u32, u31,
    sol, s3, s2, s1, out_buf, out_t,
    load_sem, send_sem, recv_sem,
):
    row = lax.axis_index("prow")
    z = lax.axis_index("pcol")
    q = row // 2
    core = row % 2
    other = 1 - core

    def dev(chip, c, zz):
        return (chip * 2 + c, zz)

    sibling = dev(q, other, z)

    loads = {}
    n_load = [0]

    def load(name, src, dst):
        copy = pltpu.make_async_copy(src, dst, load_sem.at[n_load[0]])
        n_load[0] += 1
        copy.start()
        loads[name] = copy

    load("linv", linv_hbm.at[:, 0], linv)
    load("rhs", rhs_hbm.at[:, 0], rhs)
    for p in (2, 0, 5, 4, 1, 3):
        load(("l", p), lower_hbm.at[p, 0], lower.at[p])
    load("uinv", uinv_hbm.at[:, 0], uinv.at[core])
    load("upper", upper_hbm.at[:, 0], upper)

    plane = q // 2
    x, y, qb = q // 4, q % 4, q % 2
    turn = (z - plane + 9) % 8
    flag = 1 - turn // 4
    hx = (x + 3 + 2 * (1 - flag) - turn + 8) % 4
    hy = (y + flag * (2 * qb - 1) + 4) % 4
    home_chip = hx * 4 + hy
    dx = (x - z // 2 + 4) % 4
    dy = (y - 2 * (z % 2) + 4) % 4
    src_qb = ((dy + 1) % 4) // 2
    src_v = 1 - dy // 2
    src_turn = 4 * src_v + (3 + 2 * src_v - dx + 4) % 4
    src_z = (src_turn + 7 + z) % 8
    src_chip = 2 * z + src_qb
    slot = src_qb * 8 + src_z

    barrier = pltpu.get_barrier_semaphore()

    def greet(device):
        pl.semaphore_signal(barrier, inc=1, device_id=device, device_id_type=MESH)

    def greet_plane(d, _):
        greet(dev((q + d) % CHIPS, core, z))
        return 0

    def greet_z(d, _):
        greet(dev(q, core, (z + d) % NZ))
        return 0

    def greet_cross(d, _):
        greet(dev(q, other, (z + d) % NZ))
        return 0

    def greet_move(d, _):
        greet(dev(8 * core + (q + d) % 8, q % 2, q // 2))
        return 0

    own_move = jnp.logical_and(jnp.logical_and(z == q // 2, core == q % 2), core == q // 8)
    lax.fori_loop(1, 8, greet_move, 0)

    @pl.when(jnp.logical_not(own_move))
    def _():
        greet_move(0, 0)

    greet(dev(src_chip, core, src_z))
    greet(dev(src_chip, other, src_z))
    lax.fori_loop(0, NZ, greet_cross, 0)
    lax.fori_loop(1, CHIPS, greet_plane, 0)
    lax.fori_loop(1, NZ, greet_z, 0)

    sent = []

    def remote(src, dst, sem, device):
        pltpu.make_async_remote_copy(
            src_ref=src, dst_ref=dst, send_sem=send_sem.at[sem], recv_sem=recv_sem.at[sem],
            device_id=device, device_id_type=MESH,
        ).start()

    def wait_recv(sem, ref):
        pltpu.make_async_copy(ref, ref, recv_sem.at[sem]).wait()

    sems = {}

    def new_sem(name):
        sems[name] = len(sems)
        return sems[name]

    def to_sibling(name, src, dst):
        sem = new_sem(name)
        remote(src, dst, sem, sibling)
        sent.append((sem, src))

    def plane_gather(name, src, buf, at):
        sem = new_sem(name)

        def body(d, _):
            remote(src, buf.at[at], sem, dev((q + d) % CHIPS, core, z))
            return 0

        lax.fori_loop(1, CHIPS, body, 0)
        buf[at] = src[...]
        sent.append((sem, buf.at[pl.ds(0, 15)] if len(buf.shape) == 4 else buf.at[pl.ds(0, 30)]))

    def plane_wait(name, buf):
        wait_recv(sems[name], buf.at[pl.ds(0, 15)] if len(buf.shape) == 4 else buf.at[pl.ds(0, 30)])

    def z_exchange(name, src_of, buf, at):
        sem = new_sem(name)

        def body(d, _):
            zz = (z + d) % NZ
            remote(src_of(zz), buf.at[at], sem, dev(q, core, zz))
            return 0

        lax.fori_loop(1, NZ, body, 0)
        sent.append((sem, buf.at[pl.ds(0, 7)]))

    loads["linv"].wait()
    loads["rhs"].wait()

    def make_g(h):
        g_all[h] = jnp.dot(linv[h], rhs[h], preferred_element_type=F32).T.astype(BF16)

    def make_m(p, dst, first):
        if first:
            loads[("l", p)].wait()
        for k in range(4):
            weight = mask[p, row, 4 * z + k].astype(F32)
            dst[k] = (jnp.dot(linv[ROW_OF[p]], lower[p, k], preferred_element_type=F32) * weight).astype(BF16)

    def compress_upper(n):
        p = UORD[n]
        found = jnp.int32(0)
        at = jnp.int32(0)
        for k in range(4):
            bit = mask[p, 4 * z + k, row]
            found = found + bit
            at = at + k * bit
        block = jnp.dot(uinv[core, UROW[n]], upper[p, at], preferred_element_type=F32) * found.astype(F32)
        ucand[n] = block.astype(BF16)

    def move_to_sibling(i):
        to_sibling(("mov", i), mov.at[i, pl.ds(2 * other, 2)], mov_sib.at[i])

    def combine(i):
        wait_recv(sems[("mov", i)], mov_sib.at[i])
        for e in range(2):
            comb[i, e] = mov[i, 2 * core + e] + mov_sib[i, e]
        sem = new_sem(("rs", i))

        def body(d, _):
            chip = (q + d) % CHIPS
            rows = pl.ds(pl.multiple_of(chip * W, W), W)
            remote(comb.at[i, :, rows], rs_buf.at[i, q], sem, dev(chip, core, z))
            return 0

        lax.fori_loop(1, CHIPS, body, 0)
        rs_buf[i, q] = comb[i, :, pl.ds(pl.multiple_of(q * W, W), W)]
        sent.append((sem, rs_buf.at[i, pl.ds(0, 15)]))

    def spread(i):
        wait_recv(sems[("rs", i)], rs_buf.at[i, pl.ds(0, 15)])
        total = rs_buf[i, 0].astype(F32)
        for s in range(1, CHIPS):
            total = total + rs_buf[i, s].astype(F32)
        piece[i] = total.astype(BF16)
        sem = new_sem(("lact", i))
        chip = 2 * z + core

        def body(d, _):
            remote(piece.at[i], lact.at[i, q // 8, q % 8], sem, dev(chip, q // 8, (z + d) % NZ))
            return 0

        lax.fori_loop(1, NZ, body, 0)

        @pl.when(own_move)
        def _():
            lact[i, q // 8, q % 8] = piece[i]

        @pl.when(jnp.logical_not(own_move))
        def _():
            body(0, 0)

        return sem

    def wait_moved(sem_ref, i):
        @pl.when(own_move)
        def _():
            ref = lact.at[i, 0, pl.ds(0, 7)]
            pltpu.make_async_copy(ref, ref, sem_ref).wait()

        @pl.when(jnp.logical_not(own_move))
        def _():
            ref = lact.at[i, 0]
            pltpu.make_async_copy(ref, ref, sem_ref).wait()

    spread_sems = {}

    def pass_moved(i):
        wait_moved(recv_sem.at[spread_sems[i]], i)
        to_sibling(("ls", i), lact.at[i, core], lact.at[i, core])

    def moved_ready(i):
        wait_recv(sems[("ls", i)], lact.at[i, 0])

    def products(i):
        wait_recv(sems[("m", i)], first_m.at[0, 0])
        for e in range(2):
            total = None
            for k in range(4):
                cols = x0[8 * (k // 2):8 * (k // 2) + 8, k % 2].reshape(128, B)
                term = dot_nt(cols, first_m[e, i, k])
                total = term if total is None else total + term
            part[i, :, e] = total.astype(BF16).reshape(NZ, W, B)

    def send_products(i):
        z_exchange(("z", i), lambda zz: part.at[i, zz], zsum.at[i], z)
        zsum[i, z] = part[i, z]

    def z_total(i):
        wait_recv(sems[("z", i)], zsum.at[i, pl.ds(0, 7)])
        total = zsum[i, 0].astype(F32)
        for s in range(1, NZ):
            total = total + zsum[i, s].astype(F32)
        return total

    def pushed(buf, p):
        def body(t, carry):
            for j in [t * 8 + u for u in range(8)]:
                val = buf[j].astype(F32)
                carry = tuple(carry[e] + val * mask[p, 2 * q + e, j].astype(F32) for e in range(2))
            return carry

        zero = jnp.zeros((W, B), F32)
        return lax.fori_loop(0, 4, body, (zero, zero))

    def push(name, level, i, slot_, buf):
        for e in range(2):
            block = lact[i, :, :, e].reshape(B, B)
            u_src[slot_, e] = dot_nt(fv[level, e], block).astype(BF16)
        plane_gather(name, u_src.at[slot_], buf, pl.ds(2 * q, 2))

    def upper_rows(shift):
        return pl.ds(pl.multiple_of((z + NZ + shift) % NZ * 32, 32), 32)

    def ring_send(way, n, src):
        sem = new_sem(("ring", way, n))
        buf = (ring_r if way > 0 else ring_l).at[n]
        remote(src, buf, sem, dev(q, core, (z + NZ + way) % NZ))
        sent.append((sem, buf))

    def ring_start():
        ring_send(1, 0, ucand.at[:, upper_rows(4)])
        ring_send(-1, 0, ucand.at[:, upper_rows(-3)])

    def ring_step(n):
        wait_recv(sems[("ring", 1, n - 1)], ring_r.at[n - 1])
        sum_r[n - 1] = ring_r[n - 1] + ucand[:, upper_rows(4 - n)]
        ring_send(1, n, sum_r.at[n - 1])
        if n < 3:
            wait_recv(sems[("ring", -1, n - 1)], ring_l.at[n - 1])
            sum_l[n - 1] = ring_l[n - 1] + ucand[:, upper_rows(n - 3)]
            ring_send(-1, n, sum_l.at[n - 1])

    def ring_end():
        wait_recv(sems[("ring", 1, 3)], ring_r.at[3])
        wait_recv(sems[("ring", -1, 2)], ring_l.at[2])
        upiece[...] = ring_r[3] + ring_l[2] + ucand[:, upper_rows(0)]

    uacts = (uact0, uact1, uact2)

    def spread_upper(n):
        lo, hi = UGROUPS[n]
        uact = uacts[n]
        sem = new_sem(("ua", n))

        def body(d, _):
            remote(upiece.at[pl.ds(lo, hi - lo)], uact.at[core, z], sem, dev(q, core, (z + d) % NZ))
            return 0

        lax.fori_loop(1, NZ, body, 0)
        uact[core, z] = upiece[lo:hi]
        sent.append((sem, uact.at[0, pl.ds(0, 7)]))

    def pass_upper(n):
        wait_recv(sems[("ua", n)], uacts[n].at[0, pl.ds(0, 7)])
        to_sibling(("us", n), uacts[n].at[core], uacts[n].at[core])

    def upper_ready(n):
        wait_recv(sems[("us", n)], uacts[n].at[0])

    make_g(0)
    make_m(2, mov.at[0], True)
    make_m(0, first_m.at[core, 0], True)
    for h in range(1, LEV):
        make_g(h)
    loads["uinv"].wait()
    loads["upper"].wait()
    for n in range(NPAIR):
        compress_upper(n)
    pl.semaphore_wait(barrier, 40 - own_move.astype(jnp.int32))

    sem = new_sem("home")
    mine = pl.ds(pl.multiple_of(core * 128 + z * W, W), W)
    yours = pl.ds(pl.multiple_of(other * 128 + z * W, W), W)
    remote(g_all.at[0, mine], home.at[core], sem, dev(home_chip, core, plane))
    remote(g_all.at[0, yours], home.at[core], sem, dev(home_chip, other, plane))
    sent.append((sem, home))
    move_to_sibling(0)
    to_sibling(("m", 0), first_m.at[core, 0], first_m.at[core, 0])
    to_sibling("g", g_all.at[:, yours], g_home.at[core])
    ring_start()
    g_home[core] = g_all[:, mine]
    for i in (1, 2):
        make_m(MOVED[i], mov.at[i], True)
        move_to_sibling(i)
    combine(0)

    wait_recv(sems["home"], home)
    plane_gather("x0", home, x0, slot)
    to_sibling("uinv", uinv.at[core], uinv.at[core])
    ring_step(1)
    for i in (1, 2):
        make_m(FIRST[i], first_m.at[core, i], True)
        to_sibling(("m", i), first_m.at[core, i], first_m.at[core, i])
    spread_sems[0] = spread(0)
    ring_step(2)
    combine(1)
    plane_wait("x0", x0)
    products(0)
    send_products(0)
    combine(2)
    ring_step(3)
    products(1)
    send_products(1)
    products(2)
    spread_sems[1] = spread(1)
    pass_moved(0)
    wait_recv(sems["g"], g_home.at[0])
    for e in range(2):
        fv[0, e] = g_home[e, 0]
    spread_sems[2] = spread(2)
    moved_ready(0)
    base = z_total(0)

    for e in range(2):
        fv[1, e] = (g_home[e, 1].astype(F32) - base[e]).astype(BF16)
    push("u21", 1, 0, 0, u21)
    ring_end()
    base = g_home[:, 2].astype(F32) - z_total(1)
    pass_moved(1)
    plane_wait("u21", u21)
    low, high = pushed(u21, 2)
    fv[2, 0] = (base[0] - low).astype(BF16)
    fv[2, 1] = (base[1] - high).astype(BF16)
    send_products(2)
    moved_ready(1)
    push("u32", 2, 1, 2, u32)
    pass_moved(2)
    moved_ready(2)
    push("u31", 1, 2, 1, u31)
    for n in range(3):
        spread_upper(n)
    base = g_home[:, 3].astype(F32) - z_total(2)
    plane_wait("u32", u32)
    low, high = pushed(u32, 5)
    plane_wait("u31", u31)
    low1, high1 = pushed(u31, 4)
    fv[3, 0] = (base[0] - low1 - low).astype(BF16)
    fv[3, 1] = (base[1] - high1 - high).astype(BF16)

    wait_recv(sems["uinv"], uinv.at[0])

    def own_term(level, e):
        return dot_nt(fv[level, e], uinv[e, level])

    def above(buf, n):
        group = sum(n >= lo for lo, _ in UGROUPS) - 1
        p = UORD[n]

        def body(t, chosen):
            for j in [t * 8 + u for u in range(8)]:
                val = buf[j].astype(F32)
                chosen = tuple(jnp.where(mask[p, j, 2 * q + e] == 1, val, chosen[e]) for e in range(2))
            return chosen

        zero = jnp.zeros((W, B), F32)
        chosen = lax.fori_loop(0, 4, body, (zero, zero))
        blocks = [uacts[group][e, :, n - UGROUPS[group][0]].reshape(B, B) for e in range(2)]
        return [dot_nt(chosen[e].astype(BF16), blocks[e]) for e in range(2)]

    def gather_level(level, buf):
        plane_gather(("s", level), sol.at[level], buf, pl.ds(2 * q, 2))

    def publish(level):
        sem = new_sem(("out", level))
        at = core * 8 + z

        def body(d, _):
            remote(sol.at[level, core], out_buf.at[level, at], sem, dev(q, core, (z + d) % NZ))
            return 0

        def cross(d, _):
            remote(sol.at[level, other], out_buf.at[level, at], sem, dev(q, other, (z + d) % NZ))
            return 0

        lax.fori_loop(1, NZ, body, 0)
        lax.fori_loop(0, NZ, cross, 0)
        out_buf[level, at] = sol[level, core]
        sent.append((sem, out_buf.at[level, pl.ds(0, 15)]))

    stores = []

    def finish(level):
        wait_recv(sems[("out", level)], out_buf.at[level, pl.ds(0, 15)])
        out_t[level] = out_buf[level].reshape(B, B).astype(F32).T.astype(BF16)
        copy = pltpu.make_async_copy(out_t.at[level], out_hbm.at[level, 0], load_sem.at[n_load[0]])
        n_load[0] += 1
        copy.start()
        stores.append(copy)

    for e in range(2):
        sol[3, e] = own_term(3, e).astype(BF16)
    gather_level(3, s3)
    rest = [own_term(2, e) for e in range(2)]
    pass_upper(0)
    upper_ready(0)
    plane_wait(("s", 3), s3)
    terms = above(s3, 0)
    for e in range(2):
        sol[2, e] = (rest[e] - terms[e]).astype(BF16)
    gather_level(2, s2)
    pass_upper(1)
    upper_ready(1)
    publish(3)
    terms = above(s3, 2)
    rest = [own_term(1, e) - terms[e] for e in range(2)]
    plane_wait(("s", 2), s2)
    terms = above(s2, 1)
    for e in range(2):
        sol[1, e] = (rest[e] - terms[e]).astype(BF16)
    gather_level(1, s1)
    publish(2)
    pass_upper(2)
    publish(1)
    upper_ready(2)
    terms = above(s3, 5)
    more = above(s2, 4)
    rest = [own_term(0, e) - terms[e] - more[e] for e in range(2)]
    plane_wait(("s", 1), s1)
    terms = above(s1, 3)
    for e in range(2):
        sol[0, e] = (rest[e] - terms[e]).astype(BF16)
    publish(0)
    finish(3)
    finish(2)
    finish(1)

    for sem, ref in sent:
        pltpu.make_async_copy(ref, ref, send_sem.at[sem]).wait()

    for i in range(3):
        wait_moved(send_sem.at[spread_sems[i]], i)

    finish(0)
    for copy in stores:
        copy.wait()


def per_device(right_sides, lower_diag_inverse, upper_diag_inverse, lower_blocks, upper_blocks, block_mask):
    def vmem(*shape):
        return pltpu.VMEM(shape, BF16)

    anywhere = pl.BlockSpec(memory_space=pl.ANY)
    hbm = pl.BlockSpec(memory_space=pltpu.HBM)
    return pl.pallas_call(
        kernel,
        out_shape=jax.ShapeDtypeStruct(right_sides.shape, BF16),
        in_specs=[hbm] * 5 + [pl.BlockSpec(memory_space=pltpu.SMEM)],
        out_specs=anywhere,
        scratch_shapes=[
            vmem(LEV, B, B),
            vmem(LEV, B, B),
            vmem(2, LEV, B, B),
            vmem(NPAIR, 4, B, B),
            vmem(NPAIR, 4, B, B),
            vmem(LEV, B, B),
            vmem(2, LEV, W, B),
            vmem(2, W, B),
            vmem(CHIPS, 2, W, B),
            vmem(2, 3, 4, B, B),
            vmem(3, NZ, 2, W, B),
            vmem(3, NZ, 2, W, B),
            vmem(3, 4, B, B),
            vmem(3, 2, B, B),
            vmem(3, 2, B, B),
            vmem(3, CHIPS, 2, W, B),
            vmem(3, 2, W, B),
            vmem(3, 2, 8, 2, W, B),
            vmem(NPAIR, B, B),
            vmem(4, NPAIR, 32, B),
            vmem(3, NPAIR, 32, B),
            vmem(3, NPAIR, 32, B),
            vmem(2, NPAIR, 32, B),
            vmem(NPAIR, 32, B),
            vmem(2, NZ, 1, 32, B),
            vmem(2, NZ, 2, 32, B),
            vmem(2, NZ, 3, 32, B),
            vmem(LEV, 2, W, B),
            vmem(3, 2, W, B),
            vmem(32, W, B),
            vmem(32, W, B),
            vmem(32, W, B),
            vmem(LEV, 2, W, B),
            vmem(32, W, B),
            vmem(32, W, B),
            vmem(32, W, B),
            vmem(LEV, 16, W, B),
            vmem(LEV, B, B),
            pltpu.SemaphoreType.DMA((16,)),
            pltpu.SemaphoreType.DMA((48,)),
            pltpu.SemaphoreType.DMA((48,)),
        ],
        compiler_params=pltpu.CompilerParams(
            collective_id=0, has_side_effects=True, vmem_limit_bytes=532 * 2**20 // 10
        ),
        name="tree_solve",
    )(right_sides, lower_diag_inverse, upper_diag_inverse, lower_blocks, upper_blocks, block_mask)


def solution(mesh):
    in_specs = (
        P(None, "prow", None, None),
        P(None, "prow", None, None),
        P(None, "prow", None, None),
        P(None, "prow", "pcol", None, None),
        P(None, "prow", "pcol", None, None),
        P(),
    )
    return jax.shard_map(
        per_device, mesh=mesh, in_specs=in_specs, out_specs=P(None, "prow", None, None), check_vma=False
    )
```
